128 devices in a mesh: gx: 16 (over z_hi, x, core), gy: 8 (over z_lo, y).
Axes of the slice: x: 4, y: 4, z: 4 (z_hi: 2, z_lo: 2; z = z_hi * 2 + z_lo), core: 2. Of those that a mesh axis runs over, the one named last changes fastest.
Arguments:
- fields: bfloat16 [8, 64, 32, 64, 128], P(None, None, 'gx', 'gy'), may hold values from -6 to 6
- depth_kernel: bfloat16 [64, 3, 3, 3], replicated, may hold values from -1.25 to 1.25
- point_in: bfloat16 [256, 64], replicated, may hold values from -0.75 to 0.75
- point_out: bfloat16 [64, 256], replicated, may hold values from -0.375 to 0.375
- down_kernel: bfloat16 [128, 64, 2, 2, 2], replicated, may hold values from -0.25 to 0.25
- cotangent: bfloat16 [16, 8, 1, 128, 4, 8, 64], P('gx', 'gy'), may hold values from -6 to 6
Outputs:
- coarse: bfloat16 [16, 8, 1, 128, 4, 8, 64], P('gx', 'gy')
- grad_fields: bfloat16 [8, 64, 32, 64, 128], P(None, None, 'gx', 'gy')
- grad_depth_kernel: float32 [64, 3, 3, 3], replicated
- grad_point_in: float32 [256, 64], replicated
- grad_point_out: float32 [64, 256], replicated
- grad_down_kernel: float32 [128, 64, 2, 2, 2], replicated
The draws below stay inside these ranges and needn't reach their ends.
All inputs are finite; a program needn't handle non-finite values.
Results may differ from the reference program's by a relative error of at most 0.0066.
Values may be sent and summed in bfloat16 or wider, within the bound.
A program may use at most 192 MiB of HBM per device.

```python
import math
import jax
import jax.numpy as jnp
from jax import lax

C = 64
HID = 256
C2 = 128
GRIDC = 4
NZ = 128
BG = 1
SGX = 4
SGY = 2
SAMPLES = 8
NX = 32
NY = 64
XC = 4
YC = 8
ZC = 64
N_GX = 16
N_GY = 8


def levels(own_key, extent, cuts, least, largest):
    factor_of, own = 1.0, jax.random.fold_in(own_key, 6)
    for position, parts in cuts:
        heights = jnp.exp(jax.random.uniform(jax.random.fold_in(own, position), (parts,), jnp.float32, least / len(cuts), largest / len(cuts)))
        factor_of = factor_of * jnp.repeat(heights, extent[position] // parts).reshape([-1 if axis == position else 1 for axis in range(len(extent))])
    return factor_of


def noise(stream_key, dims, scale, bound, cuts=(), dtype=jnp.bfloat16):
    result = scale * jax.random.normal(stream_key, dims, jnp.float32)
    if cuts:
        result = result * levels(stream_key, dims, cuts, -0.22, 0.18)
    return jnp.clip(result, -bound, bound).astype(dtype)


def setup_inputs(seed: int = 0) -> dict:
    streams_of = jax.random.split(jax.random.key(seed), 7)
    fields = noise(streams_of[0], (SAMPLES, C, NX, NY, NZ), 1.0, 6.0, ((2, 16), (3, 8)))
    depth_kernel = noise(streams_of[1], (C, 3, 3, 3), 27 ** -0.5, 1.25)
    point_in = noise(streams_of[2], (HID, C), C ** -0.5, 0.75)
    point_out = noise(streams_of[3], (C, HID), HID ** -0.5, 0.375)
    down_kernel = noise(streams_of[4], (C2, C, 2, 2, 2), (8 * C) ** -0.5, 0.25)
    cotangent = noise(streams_of[5], (N_GX, N_GY, BG, C2, XC, YC, ZC), 1.0, 6.0, ((0, 16), (1, 8)))
    return {"fields": fields, "depth_kernel": depth_kernel, "point_in": point_in, "point_out": point_out, "down_kernel": down_kernel, "cotangent": cotangent}


def gelu_slope(values):
    outputs, pullback = jax.vjp(jax.nn.gelu, values)
    return pullback(jnp.ones_like(outputs))[0]

def depth_conv(padded, weights, span_x, span_y, span_z):
    summed = jnp.zeros(padded.shape[:-3] + (span_x, span_y, span_z), jnp.float32)
    for offset_x in range(3):
        for offset_y in range(3):
            for offset_z in range(3):
                factor = weights[:, offset_x, offset_y, offset_z].astype(jnp.float32)[:, None, None, None]
                window = padded[..., offset_x:offset_x + span_x, offset_y:offset_y + span_y, offset_z:offset_z + span_z]
                summed = summed + factor * window.astype(jnp.float32)
    return summed

def per_sample(sample_field, sample_grad, depth_kernel, point_in, point_out, down_kernel):
    padded = jnp.pad(sample_field, ((0, 0), (1, 1), (1, 1), (1, 1)))
    depth_out = depth_conv(padded, depth_kernel, NX, NY, NZ).astype(jnp.bfloat16)
    flat_depth = depth_out.reshape(C, -1)
    preact = jnp.dot(point_in, flat_depth, preferred_element_type=jnp.float32)
    active = jax.nn.gelu(preact).astype(jnp.bfloat16)
    merged = (sample_field.reshape(C, -1).astype(jnp.float32) + jnp.dot(point_out, active, preferred_element_type=jnp.float32)).astype(jnp.bfloat16)
    patches = merged.reshape(C, NX // 2, 2, NY // 2, 2, NZ // 2, 2).transpose(0, 2, 4, 6, 1, 3, 5).reshape(C * 8, -1)
    down_mat = down_kernel.reshape(C2, C * 8)
    reduced = jnp.dot(down_mat, patches, preferred_element_type=jnp.float32).astype(jnp.bfloat16)
    grad_down = sample_grad.reshape(C2, -1)
    grad_patch = jnp.dot(down_mat.T, grad_down, preferred_element_type=jnp.float32)
    grad_merged = grad_patch.reshape(C, 2, 2, 2, NX // 2, NY // 2, NZ // 2).transpose(0, 4, 1, 5, 2, 6, 3).reshape(C, -1).astype(jnp.bfloat16)
    grad_downw = jnp.dot(grad_down, patches.T, preferred_element_type=jnp.float32)
    grad_active = jnp.dot(point_out.T, grad_merged, preferred_element_type=jnp.float32)
    grad_pre = (grad_active * gelu_slope(preact)).astype(jnp.bfloat16)
    grad_outw = jnp.dot(grad_merged, active.T, preferred_element_type=jnp.float32)
    grad_inw = jnp.dot(grad_pre, flat_depth.T, preferred_element_type=jnp.float32)
    grad_depth = jnp.dot(point_in.T, grad_pre, preferred_element_type=jnp.float32).astype(jnp.bfloat16).reshape(C, NX, NY, NZ)
    grad_pad = jnp.pad(grad_depth, ((0, 0), (1, 1), (1, 1), (1, 1)))
    adjoint = depth_conv(grad_pad, depth_kernel[:, ::-1, ::-1, ::-1], NX, NY, NZ)
    grad_field = (grad_merged.reshape(C, NX, NY, NZ).astype(jnp.float32) + adjoint).astype(jnp.bfloat16)
    columns = []
    for offset_x in range(3):
        for offset_y in range(3):
            for offset_z in range(3):
                window = padded[:, offset_x:offset_x + NX, offset_y:offset_y + NY, offset_z:offset_z + NZ]
                columns.append(lax.optimization_barrier(jnp.sum(grad_depth.astype(jnp.float32) * window.astype(jnp.float32), axis=(1, 2, 3))))
    grad_depthw = jnp.stack(columns, axis=1).reshape(C, 3, 3, 3)
    return (reduced.reshape(C2, NX // 2, NY // 2, NZ // 2), grad_field, grad_depthw, grad_inw, grad_outw, grad_downw.reshape(C2, C, 2, 2, 2))

def reference(fields, depth_kernel, point_in, point_out, down_kernel, cotangent):
    fine_grad = cotangent.reshape(GRIDC, SGX, GRIDC, SGY, BG, C2, XC, YC, ZC).transpose(1, 3, 4, 5, 0, 6, 2, 7, 8).reshape(SAMPLES, C2, NX // 2, NY // 2, NZ // 2)

    def runner(inputs):
        return per_sample(inputs[0], inputs[1], depth_kernel, point_in, point_out, down_kernel)
    reduced, grad_fields, grad_depthw, grad_inw, grad_outw, grad_downw = lax.map(runner, (fields, fine_grad))
    norm_scale = 1.0 / math.sqrt(SAMPLES * NX * NY * NZ)
    coarse = reduced.reshape(SGX, SGY, BG, C2, GRIDC, XC, GRIDC, YC, ZC).transpose(4, 0, 6, 1, 2, 3, 5, 7, 8).reshape(N_GX, N_GY, BG, C2, XC, YC, ZC)
    return (coarse, grad_fields, lax.optimization_barrier(jnp.sum(grad_depthw, axis=0)) * norm_scale, lax.optimization_barrier(jnp.sum(grad_inw, axis=0)) * norm_scale, lax.optimization_barrier(jnp.sum(grad_outw, axis=0)) * norm_scale, lax.optimization_barrier(jnp.sum(grad_downw, axis=0)) * norm_scale)
```

```python
import math

import jax
import jax.numpy as jnp
from jax import lax
from jax.experimental import pallas as pl
from jax.experimental.pallas import tpu as pltpu
from jax.sharding import PartitionSpec as P

NGX, NGY = 16, 8
S, C, HID, C2 = 8, 64, 256, 128
F32, BF16 = jnp.float32, jnp.bfloat16
MESH = pl.DeviceIdType.MESH
NN = (((1,), (0,)), ((), ()))
NT = (((1,), (1,)), ((), ()))
TN = (((0,), (0,)), ((), ()))
G0 = math.sqrt(2.0 / math.pi)
G1 = G0 * 0.044715
ROWS = 384 // NGX
SCALE = 1.0 / math.sqrt(8 * 32 * 64 * 128)


def dot(a, b, dims=NN):
    return lax.dot_general(a, b, dims, preferred_element_type=F32)


def taps(grid, s, j, g):
    sides = []
    for yy in range(2):
        block = grid[s, :, pl.ds(2 * j + yy, 3), 16 * g : 16 * g + 16, :]
        sides.append(block.reshape(192, 128))
    return jnp.concatenate(sides, axis=1)


def shifted_sum(a0, a1, a2):
    lane = lax.broadcasted_iota(jnp.int32, a1.shape, 1)
    low = lane < 64
    near = pltpu.roll(jnp.where(low, a0, a2), 64, 1)
    far = jnp.where(low, pltpu.roll(a0, 65, 1), pltpu.roll(a2, 63, 1))
    return a1 + near + jnp.where((lane == 0) | (lane == 127), 0.0, far)


def conv(grid, mats, s, j):
    parts = [dot(mats[g], taps(grid, s, j, g)) for g in range(4)]
    result = []
    for x in range(2):
        sides = []
        for yy in range(2):
            a = [
                jnp.concatenate(
                    [p[48 * x + 16 * e : 48 * x + 16 * e + 16, 128 * yy : 128 * yy + 128] for p in parts],
                    axis=0,
                )
                for e in range(3)
            ]
            sides.append(shifted_sum(*a))
        result.append(jnp.concatenate(sides, axis=1))
    return result


def kernel(
    raw, cot, lanes, pin, pin_t, pout, pout_t, w2t,
    coarse, grad_out, sums_out, dw_out,
    fg, dg, gm, gdn, red, mats, mats_t, wacc, dwacc, swap, rs, gyb, tot, t1, t2,
    f_send, f_recv, d_send, d_recv, c_send, c_recv, r_send, r_recv,
    rs_send, rs_recv, gy_send, gy_recv, ag_send, ag_recv, t1_send, t1_recv, t2_send, t2_recv, own_sem,
):
    ix, iy = lax.axis_index("gx"), lax.axis_index("gy")
    mx, my = ix % 4, iy % 2
    mine = mx * 2 + my
    bx, by = ix - mx, iy - my

    zero = jnp.zeros((S, 10, C, 128), BF16)
    zero_y = jnp.zeros((S, 4, C, 128), BF16)
    for grid in (fg, dg):
        for cond, at in ((ix == 0, 0), (ix == NGX - 1, 3)):

            @pl.when(cond)
            def _(grid=grid, at=at):
                @pl.loop(0, S)
                def _(s):
                    grid[s, at] = jnp.zeros((10, C, 128), BF16)

        for cond, at in ((iy == 0, 0), (iy == NGY - 1, 9)):

            @pl.when(cond)
            def _(grid=grid, at=at):
                @pl.loop(0, S)
                def _(s):
                    grid[s, :, at] = jnp.zeros((4, C, 128), BF16)

    barrier = pltpu.get_barrier_semaphore()
    peers = [((ix + k) % NGX, iy) for k in range(1, NGX)]
    peers += [(ix, (iy + k) % NGY) for k in range(1, NGY)]
    peers += [((ix + p) % NGX, (iy + q) % NGY) for p in (1, NGX - 1) for q in (1, NGY - 1)]
    peers += [(bx + (mx + k) % 4, by + 1 - my) for k in range(1, 4)]
    for peer in peers:
        pl.semaphore_signal(barrier, inc=1, device_id=peer, device_id_type=MESH)
    pl.semaphore_wait(barrier, len(peers))

    def remote(src, dst, send, recv, to):
        return pltpu.make_async_remote_copy(
            src_ref=src, dst_ref=dst, send_sem=send, recv_sem=recv, device_id=to, device_id_type=MESH
        )

    def cot_copy(k):
        to = (mine + k) % 8
        tx, ty = to // 2, to % 2
        return remote(
            cot.at[tx, pl.ds(ty * 4, 4)], gdn.at[mine], c_send.at[to], c_recv.at[mine], (bx + tx, by + ty)
        )

    def cot_arrival(s):
        return remote(cot.at[0, pl.ds(0, 4)], gdn.at[s], c_send.at[s], c_recv.at[s], (ix, iy))

    for k in range(1, 8):
        cot_copy(k).start()
    gdn[mine] = cot[mx, pl.ds(my * 4, 4)]

    row = lax.broadcasted_iota(jnp.int32, (16, 192), 0)
    col = lax.broadcasted_iota(jnp.int32, (16, 192), 1)
    diag = row == col % 16
    for m, (to, base) in enumerate(((mats, 0), (mats_t, 24))):
        for g in range(4):
            for q in range(6):
                line = lanes[base + 6 * g + q : base + 6 * g + q + 1, :]
                to[g, 16 * q : 16 * q + 16] = jnp.where(diag, line, 0.0).astype(BF16)
    wacc[...] = jnp.zeros_like(wacc)
    dwacc[...] = jnp.zeros_like(dwacc)

    zi = lax.broadcasted_iota(jnp.int32, (128, 128), 0)
    li = lax.broadcasted_iota(jnp.int32, (128, 128), 1)
    perm = (zi == jnp.where(li < 64, 2 * li, 2 * li - 127)).astype(BF16)

    def rims(grid, s, send, recv):
        whole, inner = pl.ds(1, 8), pl.ds(1, 2)
        west, east, south, north = ix > 0, ix < NGX - 1, iy > 0, iy < NGY - 1
        listed = [
            (west, east, (ix - 1, iy), (1, whole), (3, whole)),
            (east, west, (ix + 1, iy), (2, whole), (0, whole)),
            (south, north, (ix, iy - 1), (inner, 1), (inner, 9)),
            (north, south, (ix, iy + 1), (inner, 8), (inner, 0)),
            (west & south, east & north, (ix - 1, iy - 1), (1, 1), (3, 9)),
            (west & north, east & south, (ix - 1, iy + 1), (1, 8), (3, 0)),
            (east & south, west & north, (ix + 1, iy - 1), (2, 1), (0, 9)),
            (east & north, west & south, (ix + 1, iy + 1), (2, 8), (0, 0)),
        ]
        return [
            (goes, comes, remote(grid.at[(s, *src)], grid.at[(s, *dst)], send.at[s, d], recv.at[s, d], to))
            for d, (goes, comes, to, src, dst) in enumerate(listed)
        ]

    def send_rims(grid, s, send, recv):
        for goes, _, copy in rims(grid, s, send, recv):
            pl.when(goes)(copy.start)

    def await_rims(grid, s, send, recv):
        for _, comes, copy in rims(grid, s, send, recv):
            pl.when(comes)(copy.wait_recv)

    @pl.loop(0, S)
    def _(s):
        for h in range(4):
            block = raw[s, 16 * h : 16 * h + 16].reshape(256, 128)
            turned = dot(block, perm).reshape(16, 16, 128)
            turned = jnp.swapaxes(turned, 0, 1).astype(BF16)
            for x in range(2):
                fg[s, 1 + x, 1:9, 16 * h : 16 * h + 16, :] = turned[8 * x : 8 * x + 8]
        send_rims(fg, s, f_send, f_recv)

    def coarse_copy(s):
        return remote(
            red.at[s], coarse.at[mx, pl.ds(my * 4, 4)], r_send.at[s], r_recv.at[mine], (bx + s // 2, by + s % 2)
        )

    def coarse_arrival(s):
        return remote(
            red.at[s], coarse.at[s // 2, pl.ds(s % 2 * 4, 4)], r_send.at[s], r_recv.at[s], (ix, iy)
        )

    def own_coarse():
        return pltpu.make_async_copy(red.at[mine], coarse.at[mx, pl.ds(my * 4, 4)], own_sem)

    @pl.loop(0, S)
    def _(s):
        await_rims(fg, s, f_send, f_recv)

        @pl.when(s != mine)
        def _():
            cot_arrival(s).wait_recv()

        @pl.loop(0, 4)
        def _(j):
            down = gdn[s, j]
            none = jnp.zeros_like(down)
            down = jnp.concatenate(
                [jnp.concatenate([down, none], axis=1), jnp.concatenate([none, down], axis=1)], axis=0
            )
            gm_all = dot(w2t[...], down, NT).astype(BF16)
            depth = conv(fg, mats, s, j)
            stacked = []
            for x in range(2):
                dep = depth[x].astype(BF16)
                gm_x = jnp.concatenate(
                    [gm_all[128 * x : 128 * x + 64], gm_all[128 * x + 64 : 128 * x + 128]], axis=1
                )
                pre = dot(pin[...], dep)
                sq = pre * pre
                t = jnp.tanh(pre * (G0 + G1 * sq))
                half = 0.5 * pre
                act = (half + half * t).astype(BF16)
                own = jnp.concatenate(
                    [fg[s, 1 + x, 1 + 2 * j + yy].astype(F32) for yy in range(2)], axis=1
                )
                merged = (own + dot(pout[...], act)).astype(BF16)
                stacked += [merged[:, :128], merged[:, 128:]]
                slope = 0.5 + 0.5 * t + half * (1.0 - t * t) * (G0 + 3 * G1 * sq)
                gpre = (dot(pout_t[...], gm_x) * slope).astype(BF16)
                wacc[0:64] += dot(gm_x, act, NT)
                wacc[64:128] += dot(dep, gpre, NT)
                gdep = dot(pin_t[...], gpre).astype(BF16)
                for yy in range(2):
                    dg[s, 1 + x, 1 + 2 * j + yy] = gdep[:, 128 * yy : 128 * yy + 128]
                    gm[s, x, 2 * j + yy] = gm_x[:, 128 * yy : 128 * yy + 128]
            stacked = jnp.concatenate(stacked, axis=0)
            wacc[128:384] += dot(stacked, down)
            both = dot(stacked, w2t[...], TN)
            red[s, j] = (both[:64, :128] + both[64:, 128:]).astype(BF16)

        send_rims(dg, s, d_send, d_recv)

        @pl.when(s != mine)
        def _():
            coarse_copy(s).start()

    own_coarse().start()

    def rs_copy(k):
        to = (ix + k) % NGX
        return remote(wacc.at[pl.ds(to * ROWS, ROWS)], rs.at[ix], rs_send.at[k], rs_recv.at[NGX - k], (to, iy))

    def gy_copy(k):
        to = (iy + k) % NGY
        return remote(gyb.at[iy], gyb.at[iy], gy_send.at[k], gy_recv.at[NGY - k], (ix, to))

    def ag_copy(k):
        to = (ix + k) % NGX
        return remote(tot.at[ix], tot.at[ix], ag_send.at[k], ag_recv.at[NGX - k], (to, iy))

    def t1_copy(k):
        to = (ix + k) % NGX
        return remote(t1.at[ix], t1.at[ix], t1_send.at[k], t1_recv.at[NGX - k], (to, iy))

    def t2_copy(k):
        to = (iy + k) % NGY
        return remote(t2.at[iy], t2.at[iy], t2_send.at[k], t2_recv.at[NGY - k], (ix, to))

    def arrival(buffer, slot, send, recv, k):
        return remote(buffer.at[slot], buffer.at[slot], send.at[k], recv.at[k], (ix, iy))

    def total(buffer, n):
        result = buffer[0]
        for q in range(1, n):
            result = result + buffer[q]
        return result

    for k in range(1, NGX):
        rs_copy(k).start()
    rs[ix] = wacc[pl.ds(pl.multiple_of(ix * ROWS, 8), ROWS)]

    @pl.loop(0, S)
    def _(s):
        await_rims(dg, s, d_send, d_recv)

        @pl.loop(0, 4)
        def _(j):
            adjoint = conv(dg, mats_t, s, j)
            lefts = []
            for x in range(2):
                sides = []
                for yy in range(2):
                    at = 2 * j + yy
                    summed = gm[s, x, at].astype(F32) + adjoint[x][:, 128 * yy : 128 * yy + 128]
                    back = dot(summed.astype(BF16), perm, NT)
                    swap[8 * x + at] = back
                    here = dg[s, 1 + x, 1 + at].astype(F32)
                    none = jnp.zeros_like(here)
                    sides.append((shifted_sum(none, none, here), here, shifted_sum(here, none, none)))
                for e in range(3):
                    lefts.append(jnp.concatenate([sides[0][e], sides[1][e]], axis=1).astype(BF16))
            for g in range(4):
                left = jnp.concatenate([m[16 * g : 16 * g + 16] for m in lefts], axis=0)
                dwacc[g] += dot(left, taps(fg, s, j, g), NT)

        for h in range(4):
            turned = jnp.swapaxes(swap[:, 16 * h : 16 * h + 16, :], 0, 1)
            grad_out[s, 16 * h : 16 * h + 16] = turned.astype(BF16)

        @pl.when(s == 2)
        def _():
            for k in range(1, NGX):
                arrival(rs, (ix + k) % NGX, rs_send, rs_recv, k).wait_recv()
            gyb[iy] = total(rs, NGX)
            for k in range(1, NGY):
                gy_copy(k).start()

        @pl.when(s == 5)
        def _():
            for k in range(1, NGY):
                arrival(gyb, (iy + k) % NGY, gy_send, gy_recv, k).wait_recv()
            tot[ix] = total(gyb, NGY) * SCALE
            for k in range(1, NGX):
                ag_copy(k).start()

    lines = []
    for g in range(4):
        for q in range(6):
            block = jnp.where(diag, dwacc[g, 16 * q : 16 * q + 16, :], 0.0)
            lines.append(jnp.sum(block, axis=0, keepdims=True))
    t1[ix] = jnp.concatenate(lines, axis=0)
    for k in range(1, NGX):
        t1_copy(k).start()
    for k in range(1, NGX):
        arrival(t1, (ix + k) % NGX, t1_send, t1_recv, k).wait_recv()
    t2[iy] = total(t1, NGX)
    for k in range(1, NGY):
        t2_copy(k).start()
    for k in range(1, NGX):
        arrival(tot, (ix + k) % NGX, ag_send, ag_recv, k).wait_recv()
    sums_out[...] = tot[...]
    for k in range(1, NGY):
        arrival(t2, (iy + k) % NGY, t2_send, t2_recv, k).wait_recv()
    dw_out[...] = total(t2, NGY) * SCALE

    own_coarse().wait()

    @pl.loop(0, S)
    def _(s):
        @pl.when(s != mine)
        def _():
            coarse_arrival(s).wait_recv()
            coarse_copy(s).wait_send()

        for grid, send, recv in ((fg, f_send, f_recv), (dg, d_send, d_recv)):
            for goes, _, copy in rims(grid, s, send, recv):
                pl.when(goes)(copy.wait_send)

    for k in range(1, 8):
        cot_copy(k).wait_send()
    for k in range(1, NGX):
        rs_copy(k).wait_send()
        ag_copy(k).wait_send()
        t1_copy(k).wait_send()
    for k in range(1, NGY):
        gy_copy(k).wait_send()
        t2_copy(k).wait_send()


def per_device(fields, depth_kernel, point_in, point_out, down_kernel, cotangent):
    raw = fields.reshape(S, C, 16, 128)
    cot = cotangent[0, 0, 0].transpose(1, 2, 3, 0)
    w = depth_kernel.astype(F32).transpose(1, 2, 3, 0)
    w = jnp.stack([w, w[::-1, ::-1, ::-1]])
    w = jnp.stack([jnp.pad(w, ((0, 0), (x, 1 - x), (0, 0), (0, 0), (0, 0))) for x in range(2)])
    lanes = w.reshape(2, 2, 4, 3, 3, 4, 16).transpose(1, 5, 0, 4, 2, 3, 6).reshape(48, 192)
    w2t = down_kernel.transpose(2, 3, 1, 4, 0).reshape(256, 256)
    vmem = pl.BlockSpec(memory_space=pltpu.VMEM)
    dma = pltpu.SemaphoreType.DMA
    coarse, grad, sums, dw = pl.pallas_call(
        kernel,
        out_shape=(
            jax.ShapeDtypeStruct((4, 8, 64, 128), BF16),
            jax.ShapeDtypeStruct((S, C, 16, 128), BF16),
            jax.ShapeDtypeStruct((NGX, ROWS, 256), F32),
            jax.ShapeDtypeStruct((24, 192), F32),
        ),
        in_specs=[vmem] * 8,
        out_specs=[vmem] * 4,
        scratch_shapes=[
            pltpu.VMEM((S, 4, 10, C, 128), BF16),
            pltpu.VMEM((S, 4, 10, C, 128), BF16),
            pltpu.VMEM((S, 2, 8, C, 128), BF16),
            pltpu.VMEM((S, 4, 64, 128), BF16),
            pltpu.VMEM((S, 4, 64, 128), BF16),
            pltpu.VMEM((4, 96, 192), BF16),
            pltpu.VMEM((4, 96, 192), BF16),
            pltpu.VMEM((384, 256), F32),
            pltpu.VMEM((4, 96, 192), F32),
            pltpu.VMEM((16, C, 128), F32),
            pltpu.VMEM((NGX, ROWS, 256), F32),
            pltpu.VMEM((NGY, ROWS, 256), F32),
            pltpu.VMEM((NGX, ROWS, 256), F32),
            pltpu.VMEM((NGX, 24, 192), F32),
            pltpu.VMEM((NGY, 24, 192), F32),
            dma((S, 8)), dma((S, 8)), dma((S, 8)), dma((S, 8)),
            dma((8,)), dma((8,)), dma((8,)), dma((8,)),
            dma((NGX,)), dma((NGX,)), dma((NGY,)), dma((NGY,)), dma((NGX,)), dma((NGX,)),
            dma((NGX,)), dma((NGX,)), dma((NGY,)), dma((NGY,)),
            dma,
        ],
        compiler_params=pltpu.CompilerParams(
            collective_id=0, has_side_effects=True, vmem_limit_bytes=56 * 2**20
        ),
    )(raw, cot, lanes, point_in, point_in.T, point_out, point_out.T, w2t)
    coarse = coarse.transpose(3, 0, 1, 2)[None, None, None]
    sums = sums.reshape(384, 256)
    grad_down = sums[128:].reshape(2, 2, 64, 2, 128).transpose(4, 2, 0, 1, 3)
    dw = dw.reshape(4, 2, 3, 4, 3, 16)
    dw = dw[:, 0, :, :3] + dw[:, 1, :, 1:]
    dw = dw.transpose(0, 4, 2, 3, 1).reshape(C, 3, 3, 3)
    return coarse, grad.reshape(fields.shape), dw, sums[64:128].T, sums[:64], grad_down


def solution(mesh):
    split = P("gx", "gy", None, None, None, None, None)
    fine = P(None, None, "gx", "gy", None)
    return jax.shard_map(
        per_device,
        mesh=mesh,
        in_specs=(fine, P(), P(), P(), P(), split),
        out_specs=(split, fine, P(), P(), P(), P()),
        check_vma=False,
    )
```

```python
import math

import jax
import jax.numpy as jnp
from jax import lax
from jax.experimental import pallas as pl
from jax.experimental.pallas import tpu as pltpu
from jax.sharding import PartitionSpec as P

NGX, NGY = 16, 8
S, C, HID, C2 = 8, 64, 256, 128
F32, BF16 = jnp.float32, jnp.bfloat16
MESH = pl.DeviceIdType.MESH
NN = (((1,), (0,)), ((), ()))
NT = (((1,), (1,)), ((), ()))
TN = (((0,), (0,)), ((), ()))
G0 = math.sqrt(2.0 / math.pi)
G1 = G0 * 0.044715
HALF, PART = 448, 56
SCALE = 1.0 / math.sqrt(8 * 32 * 64 * 128)


def dot(a, b, dims=NN):
    return lax.dot_general(a, b, dims, preferred_element_type=F32)


def taps(grid, s, j, g):
    sides = []
    for yy in range(2):
        block = grid[s, :, pl.ds(2 * j + yy, 3), 16 * g : 16 * g + 16, :]
        sides.append(block.reshape(192, 128))
    return jnp.concatenate(sides, axis=1)


def shifted_sum(a0, a1, a2):
    lane = lax.broadcasted_iota(jnp.int32, a1.shape, 1)
    low = lane < 64
    near = pltpu.roll(jnp.where(low, a0, a2), 64, 1)
    far = jnp.where(low, pltpu.roll(a0, 65, 1), pltpu.roll(a2, 63, 1))
    return a1 + near + jnp.where((lane == 0) | (lane == 127), 0.0, far)


def conv(grid, mats, s, j):
    parts = [dot(mats[g], taps(grid, s, j, g)) for g in range(4)]
    result = []
    for x in range(2):
        sides = []
        for yy in range(2):
            a = [
                jnp.concatenate(
                    [p[48 * x + 16 * e : 48 * x + 16 * e + 16, 128 * yy : 128 * yy + 128] for p in parts],
                    axis=0,
                )
                for e in range(3)
            ]
            sides.append(shifted_sum(*a))
        result.append(jnp.concatenate(sides, axis=1))
    return result


def kernel(
    raw_hbm, cot, taps_in, pin_t, pout, down_in,
    coarse, grad_out, grad_in, grad_po, grad_down, dw_out,
    raw, pin, pout_t, w2t, wide,
    fg, dg, gm, gdn, red, mats, mats_t, wacc, dwacc, swap, pair, rs, gyb, tot,
    f_send, f_recv, d_send, d_recv, c_send, c_recv, r_send, r_recv,
    rs_send, rs_recv, gy_send, gy_recv, ag_send, ag_recv, pair_send, pair_recv, own_sem, in_sem,
):
    ix, iy = lax.axis_index("gx"), lax.axis_index("gy")
    mx, my = ix % 4, iy % 2
    mine = mx * 2 + my
    bx, by = ix - mx, iy - my

    def load(s):
        return pltpu.make_async_copy(raw_hbm.at[s], raw.at[s], in_sem.at[s])

    for s in range(S):
        load(s).start()

    for grid in (fg, dg):
        for cond, at in ((ix == 0, 0), (ix == NGX - 1, 3)):

            @pl.when(cond)
            def _(grid=grid, at=at):
                @pl.loop(0, S)
                def _(s):
                    grid[s, at] = jnp.zeros((10, C, 128), BF16)

        for cond, at in ((iy == 0, 0), (iy == NGY - 1, 9)):

            @pl.when(cond)
            def _(grid=grid, at=at):
                @pl.loop(0, S)
                def _(s):
                    grid[s, :, at] = jnp.zeros((4, C, 128), BF16)

    barrier = pltpu.get_barrier_semaphore()
    core, chip = ix % 2, ix // 2
    peers = [((ix + k) % NGX, iy) for k in range(2, NGX, 2)]
    peers += [(ix + 1 - 2 * core, iy), ((ix + NGX - 1 + 2 * core) % NGX, iy)]
    peers += [(ix, (iy + k) % NGY) for k in range(1, NGY)]
    peers += [((ix + p) % NGX, (iy + q) % NGY) for p in (1, NGX - 1) for q in (1, NGY - 1)]
    peers += [(bx + (mine + k) % 8 // 2, by + (mine + k) % 2) for k in range(1, 8)]
    for peer in peers:
        pl.semaphore_signal(barrier, inc=1, device_id=peer, device_id_type=MESH)

    def remote(src, dst, send, recv, to):
        return pltpu.make_async_remote_copy(
            src_ref=src, dst_ref=dst, send_sem=send, recv_sem=recv, device_id=to, device_id_type=MESH
        )

    def cot_copy(k):
        to = (mine + k) % 8
        tx, ty = to // 2, to % 2
        return remote(
            cot.at[tx, pl.ds(ty * 4, 4)], gdn.at[mine], c_send.at[to], c_recv.at[mine], (bx + tx, by + ty)
        )

    def cot_arrival(s):
        return remote(cot.at[0, pl.ds(0, 4)], gdn.at[s], c_send.at[s], c_recv.at[s], (ix, iy))

    def send_cot():
        for k in range(1, 8):
            cot_copy(k).start()

    gdn[mine] = cot[mx, pl.ds(my * 4, 4)]

    pin[...] = pin_t[...].astype(F32).T.astype(BF16)
    pout_t[...] = pout[...].astype(F32).T.astype(BF16)
    wide[...] = down_in[...].astype(F32)
    for k in range(8):
        at = 64 * (k // 2)
        w2t[at : at + 64, k % 2 * 128 : k % 2 * 128 + 128] = wide[pl.ds(k, 64, stride=8), :].astype(BF16)

    row = lax.broadcasted_iota(jnp.int32, (16, 192), 0)
    col = lax.broadcasted_iota(jnp.int32, (16, 192), 1)
    diag = row == col % 16
    tap = lax.broadcasted_iota(jnp.int32, (27, 192), 0)
    spot = lax.broadcasted_iota(jnp.int32, (27, 192), 1)
    coefficients = taps_in[...]
    for q in range(6):
        x, e = q // 3, q % 3
        a = spot // 48 - x
        at = 9 * a + 3 * (spot // 16 % 3) + e
        inside = (a >= 0) & (a <= 2)
        for to, place in ((mats, at), (mats_t, 26 - at)):
            spread = dot(coefficients, ((tap == place) & inside).astype(BF16), TN)
            for g in range(4):
                to[g, 16 * q : 16 * q + 16] = jnp.where(diag, spread[16 * g : 16 * g + 16], 0.0).astype(BF16)
    wacc[...] = jnp.zeros_like(wacc)
    dwacc[...] = jnp.zeros_like(dwacc)

    zi = lax.broadcasted_iota(jnp.int32, (128, 128), 0)
    li = lax.broadcasted_iota(jnp.int32, (128, 128), 1)
    perm = (zi == jnp.where(li < 64, 2 * li, 2 * li - 127)).astype(BF16)

    def add(at, term):
        n = term.shape[0]
        wacc[at : at + n] += term[:, :128]
        wacc[at + n : at + 2 * n] += term[:, 128:]

    def rims(grid, s, send, recv):
        whole, inner = pl.ds(1, 8), pl.ds(1, 2)
        west, east, south, north = ix > 0, ix < NGX - 1, iy > 0, iy < NGY - 1
        listed = [
            (west, east, (ix - 1, iy), (1, whole), (3, whole)),
            (east, west, (ix + 1, iy), (2, whole), (0, whole)),
            (south, north, (ix, iy - 1), (inner, 1), (inner, 9)),
            (north, south, (ix, iy + 1), (inner, 8), (inner, 0)),
            (west & south, east & north, (ix - 1, iy - 1), (1, 1), (3, 9)),
            (west & north, east & south, (ix - 1, iy + 1), (1, 8), (3, 0)),
            (east & south, west & north, (ix + 1, iy - 1), (2, 1), (0, 9)),
            (east & north, west & south, (ix + 1, iy + 1), (2, 8), (0, 0)),
        ]
        return [
            (goes, comes, remote(grid.at[(s, *src)], grid.at[(s, *dst)], send.at[s, d], recv.at[s, d], to))
            for d, (goes, comes, to, src, dst) in enumerate(listed)
        ]

    def send_rims(grid, s, send, recv):
        for goes, _, copy in rims(grid, s, send, recv):
            pl.when(goes)(copy.start)

    def await_rims(grid, s, send, recv):
        for _, comes, copy in rims(grid, s, send, recv):
            pl.when(comes)(copy.wait_recv)

    def prepare(s):
        load(s).wait()
        for h in range(4):
            block = raw[s, 16 * h : 16 * h + 16].reshape(256, 128)
            turned = dot(block, perm).reshape(16, 16, 128)
            turned = jnp.swapaxes(turned, 0, 1).astype(BF16)
            for x in range(2):
                fg[s, 1 + x, 1:9, 16 * h : 16 * h + 16, :] = turned[8 * x : 8 * x + 8]

    def coarse_copy(s):
        return remote(
            red.at[s], coarse.at[mx, pl.ds(my * 4, 4)], r_send.at[s], r_recv.at[mine], (bx + s // 2, by + s % 2)
        )

    def coarse_arrival(s):
        return remote(
            red.at[s], coarse.at[s // 2, pl.ds(s % 2 * 4, 4)], r_send.at[s], r_recv.at[s], (ix, iy)
        )

    def own_coarse():
        return pltpu.make_async_copy(red.at[mine], coarse.at[mx, pl.ds(my * 4, 4)], own_sem)

    for s in range(2):
        prepare(s)
    pl.semaphore_wait(barrier, len(peers))
    pl.when(mine < 2)(send_cot)
    for s in range(2):
        send_rims(fg, s, f_send, f_recv)

    @pl.loop(0, S)
    def _(s):
        @pl.when(s < S - 2)
        def _():
            prepare(s + 2)
            pl.when(mine == s + 2)(send_cot)
            send_rims(fg, s + 2, f_send, f_recv)

        await_rims(fg, s, f_send, f_recv)

        @pl.when(s != mine)
        def _():
            cot_arrival(s).wait_recv()

        @pl.loop(0, 4)
        def _(j):
            down = gdn[s, j]
            none = jnp.zeros_like(down)
            down = jnp.concatenate(
                [jnp.concatenate([down, none], axis=1), jnp.concatenate([none, down], axis=1)], axis=0
            )
            gm_all = dot(w2t[...], down, NT).astype(BF16)
            depth = conv(fg, mats, s, j)
            stacked, lefts = [], []
            for x in range(2):
                dep = depth[x].astype(BF16)
                gm_x = jnp.concatenate(
                    [gm_all[128 * x : 128 * x + 64], gm_all[128 * x + 64 : 128 * x + 128]], axis=1
                )
                pre_x, grad_x = dot(pin[...], dep), dot(pout_t[...], gm_x)
                acts, gpres = [], []
                for h in range(0, HID, 64):
                    pre, grad = pre_x[h : h + 64], grad_x[h : h + 64]
                    sq = pre * pre
                    t = jnp.tanh(pre * (G0 + G1 * sq))
                    up = 0.5 + 0.5 * t
                    acts.append((pre * up).astype(BF16))
                    slope = up + 0.5 * pre * (1.0 - t * t) * (G0 + 3 * G1 * sq)
                    gpres.append((grad * slope).astype(BF16))
                act, gpre = jnp.concatenate(acts, axis=0), jnp.concatenate(gpres, axis=0)
                own = jnp.concatenate(
                    [fg[s, 1 + x, 1 + 2 * j + yy].astype(F32) for yy in range(2)], axis=1
                )
                merged = (own + dot(pout[...], act)).astype(BF16)
                stacked += [merged[:, :128], merged[:, 128:]]
                add(0, dot(gm_x, act, NT))
                add(128, dot(dep, gpre, NT))
                gdep = dot(pin_t[...], gpre).astype(BF16)
                sides = []
                for yy in range(2):
                    part = gdep[:, 128 * yy : 128 * yy + 128]
                    dg[s, 1 + x, 1 + 2 * j + yy] = part
                    gm[s, x, 2 * j + yy] = gm_x[:, 128 * yy : 128 * yy + 128]
                    here = part.astype(F32)
                    none = jnp.zeros_like(here)
                    sides.append((shifted_sum(none, none, here), here, shifted_sum(here, none, none)))
                for e in range(3):
                    lefts.append(jnp.concatenate([sides[0][e], sides[1][e]], axis=1).astype(BF16))
            for g in range(4):
                left = jnp.concatenate([m[16 * g : 16 * g + 16] for m in lefts], axis=0)
                dwacc[g] += dot(left, taps(fg, s, j, g), NT)
            stacked = jnp.concatenate(stacked, axis=0)
            add(256, dot(stacked, down))
            both = dot(stacked, w2t[...], TN)
            red[s, j] = (both[:64, :128] + both[64:, 128:]).astype(BF16)

        send_rims(dg, s, d_send, d_recv)

        @pl.when(s != mine)
        def _():
            coarse_copy(s).start()

    own_coarse().start()

    spot = lax.broadcasted_iota(jnp.int32, (192, 128), 0)
    tap = lax.broadcasted_iota(jnp.int32, (192, 128), 1)
    found = jnp.zeros((C, 128), F32)
    for q in range(6):
        a = spot // 48 - q // 3
        picks = (tap == 9 * a + 3 * (spot // 16 % 3) + q % 3) & (a >= 0) & (a <= 2)
        block = jnp.concatenate(
            [jnp.where(diag, dwacc[g, 16 * q : 16 * q + 16, :], 0.0) for g in range(4)], axis=0
        )
        found += lax.dot_general(
            block, picks.astype(F32), NN, precision=lax.Precision.HIGHEST, preferred_element_type=F32
        )
    wacc[768:832] = found

    def block(start, rows):
        return pl.ds(pl.multiple_of(start, 8), rows)

    def other(k):
        return (chip + k) % 8

    def pair_copy():
        give = block((1 - core) * HALF, HALF)
        return remote(wacc.at[give], pair, pair_send.at[0], pair_recv.at[0], (ix + 1 - 2 * core, iy))

    def rs_copy(k):
        give = block(core * HALF + other(k) * PART, PART)
        return remote(wacc.at[give], rs.at[chip], rs_send.at[k], rs_recv.at[8 - k], (2 * other(k) + core, iy))

    def rs_arrival(k):
        give = block(core * HALF, PART)
        return remote(wacc.at[give], rs.at[other(k)], rs_send.at[k], rs_recv.at[k], (ix, iy))

    def gy_copy(k):
        return remote(gyb.at[iy], gyb.at[iy], gy_send.at[k], gy_recv.at[NGY - k], (ix, (iy + k) % NGY))

    def gy_arrival(k):
        slot = (iy + k) % NGY
        return remote(gyb.at[slot], gyb.at[slot], gy_send.at[k], gy_recv.at[k], (ix, iy))

    def ag_copy(k):
        rows = block(core * HALF + chip * PART, PART)
        return remote(tot.at[rows], tot.at[rows], ag_send.at[k], ag_recv.at[8 - k], (2 * other(k) + core, iy))

    def ag_arrival(k):
        rows = block(core * HALF + other(k) * PART, PART)
        return remote(tot.at[rows], tot.at[rows], ag_send.at[k], ag_recv.at[k], (ix, iy))

    def last_copy():
        rows = block(core * HALF, HALF)
        return remote(tot.at[rows], tot.at[rows], pair_send.at[1], pair_recv.at[1], (ix + 1 - 2 * core, iy))

    def last_arrival():
        rows = block((1 - core) * HALF, HALF)
        return remote(tot.at[rows], tot.at[rows], pair_send.at[1], pair_recv.at[1], (ix, iy))

    def total(buffer):
        result = buffer[0]
        for q in range(1, 8):
            result = result + buffer[q]
        return result

    pair_copy().start()

    @pl.loop(0, S)
    def _(s):
        await_rims(dg, s, d_send, d_recv)

        @pl.loop(0, 4)
        def _(j):
            adjoint = conv(dg, mats_t, s, j)
            for x in range(2):
                for yy in range(2):
                    at = 2 * j + yy
                    summed = gm[s, x, at].astype(F32) + adjoint[x][:, 128 * yy : 128 * yy + 128]
                    back = dot(summed.astype(BF16), perm, NT)
                    swap[8 * x + at] = back

        for h in range(4):
            turned = jnp.swapaxes(swap[:, 16 * h : 16 * h + 16, :], 0, 1)
            grad_out[s, 16 * h : 16 * h + 16] = turned.astype(BF16)

        @pl.when(s == 0)
        def _():
            pair_copy().wait_recv()
            wacc[block(core * HALF, HALF)] += pair[...]
            for k in range(1, 8):
                rs_copy(k).start()

        @pl.when(s == 2)
        def _():
            rs[chip] = wacc[block(core * HALF + chip * PART, PART)]
            for k in range(1, 8):
                rs_arrival(k).wait_recv()
            gyb[iy] = total(rs)
            for k in range(1, NGY):
                gy_copy(k).start()

        @pl.when(s == 4)
        def _():
            for k in range(1, NGY):
                gy_arrival(k).wait_recv()
            tot[block(core * HALF + chip * PART, PART)] = total(gyb) * SCALE
            for k in range(1, 8):
                ag_copy(k).start()

        @pl.when(s == 6)
        def _():
            for k in range(1, 8):
                ag_arrival(k).wait_recv()
            last_copy().start()

    last_arrival().wait_recv()
    for out, at in ((grad_po, 0), (grad_in, 128)):
        out[:, :128] = tot[at : at + 64]
        out[:, 128:] = tot[at + 64 : at + 128]
    for k in range(8):
        at = 256 + 256 * (k % 2) + 64 * (k // 2)
        grad_down[pl.ds(k, 64, stride=8), :] = tot[at : at + 64]
    dw_out[...] = tot[768:832].T[:27]

    own_coarse().wait()

    @pl.loop(0, S)
    def _(s):
        @pl.when(s != mine)
        def _():
            coarse_arrival(s).wait_recv()
            coarse_copy(s).wait_send()

        for grid, send, recv in ((fg, f_send, f_recv), (dg, d_send, d_recv)):
            for goes, _, copy in rims(grid, s, send, recv):
                pl.when(goes)(copy.wait_send)

    for k in range(1, 8):
        cot_copy(k).wait_send()
        rs_copy(k).wait_send()
        ag_copy(k).wait_send()
        gy_copy(k).wait_send()
    pair_copy().wait_send()
    last_copy().wait_send()


def per_device(fields, depth_kernel, point_in, point_out, down_kernel, cotangent):
    raw = fields.reshape(S, C, 16, 128)
    cot = cotangent[0, 0, 0].transpose(1, 2, 3, 0)
    taps_in = depth_kernel.transpose(1, 2, 3, 0).reshape(27, C)
    down_in = down_kernel.transpose(1, 2, 3, 4, 0).reshape(8 * C, C2)
    vmem = pl.BlockSpec(memory_space=pltpu.VMEM)
    dma = pltpu.SemaphoreType.DMA
    hbm = pl.BlockSpec(memory_space=pl.ANY)
    coarse, grad, grad_in, grad_po, grad_down, dw = pl.pallas_call(
        kernel,
        out_shape=(
            jax.ShapeDtypeStruct((4, 8, 64, 128), BF16),
            jax.ShapeDtypeStruct((S, C, 16, 128), BF16),
            jax.ShapeDtypeStruct((C, HID), F32),
            jax.ShapeDtypeStruct((C, HID), F32),
            jax.ShapeDtypeStruct((8 * C, C2), F32),
            jax.ShapeDtypeStruct((27, C), F32),
        ),
        in_specs=[hbm] + [vmem] * 5,
        out_specs=[vmem] * 6,
        scratch_shapes=[
            pltpu.VMEM((S, C, 16, 128), BF16),
            pltpu.VMEM((HID, C), BF16),
            pltpu.VMEM((HID, C), BF16),
            pltpu.VMEM((256, 256), BF16),
            pltpu.VMEM((8 * C, C2), F32),
            pltpu.VMEM((S, 4, 10, C, 128), BF16),
            pltpu.VMEM((S, 4, 10, C, 128), BF16),
            pltpu.VMEM((S, 2, 8, C, 128), BF16),
            pltpu.VMEM((S, 4, 64, 128), BF16),
            pltpu.VMEM((S, 4, 64, 128), BF16),
            pltpu.VMEM((4, 96, 192), BF16),
            pltpu.VMEM((4, 96, 192), BF16),
            pltpu.VMEM((2 * HALF, 128), F32),
            pltpu.VMEM((4, 96, 192), F32),
            pltpu.VMEM((16, C, 128), F32),
            pltpu.VMEM((HALF, 128), F32),
            pltpu.VMEM((8, PART, 128), F32),
            pltpu.VMEM((NGY, PART, 128), F32),
            pltpu.VMEM((2 * HALF, 128), F32),
            dma((S, 8)), dma((S, 8)), dma((S, 8)), dma((S, 8)),
            dma((8,)), dma((8,)), dma((8,)), dma((8,)),
            dma((8,)), dma((8,)), dma((NGY,)), dma((NGY,)), dma((8,)), dma((8,)), dma((2,)), dma((2,)),
            dma, dma((S,)),
        ],
        compiler_params=pltpu.CompilerParams(
            collective_id=0, has_side_effects=True, vmem_limit_bytes=56 * 2**20
        ),
    )(raw, cot, taps_in, point_in.T, point_out, down_in)
    coarse = coarse.transpose(3, 0, 1, 2)[None, None, None]
    grad_down = grad_down.reshape(C, 2, 2, 2, C2).transpose(4, 0, 1, 2, 3)
    dw = dw.reshape(3, 3, 3, C).transpose(3, 0, 1, 2)
    return coarse, grad.reshape(fields.shape), dw, grad_in.T, grad_po, grad_down


def solution(mesh):
    split = P("gx", "gy", None, None, None, None, None)
    fine = P(None, None, "gx", "gy", None)
    return jax.shard_map(
        per_device,
        mesh=mesh,
        in_specs=(fine, P(), P(), P(), P(), split),
        out_specs=(split, fine, P(), P(), P(), P()),
        check_vma=False,
    )
```

```python
import math

import jax
import jax.numpy as jnp
from jax import lax
from jax.experimental import pallas as pl
from jax.experimental.pallas import tpu as pltpu
from jax.sharding import PartitionSpec as P

NGX, NGY = 16, 8
S, C, HID, C2 = 8, 64, 256, 128
F32, BF16 = jnp.float32, jnp.bfloat16
MESH = pl.DeviceIdType.MESH
NN = (((1,), (0,)), ((), ()))
NT = (((1,), (1,)), ((), ()))
TN = (((0,), (0,)), ((), ()))
G0 = math.sqrt(2.0 / math.pi)
G1 = G0 * 0.044715
HALF, PART = 448, 56
SCALE = 1.0 / math.sqrt(8 * 32 * 64 * 128)


def dot(a, b, dims=NN):
    return lax.dot_general(a, b, dims, preferred_element_type=F32)


def taps(grid, s, j, g):
    sides = []
    for yy in range(2):
        block = grid[s, :, pl.ds(2 * j + yy, 3), 16 * g : 16 * g + 16, :]
        sides.append(block.reshape(192, 128))
    return jnp.concatenate(sides, axis=1)


def shifted_sum(a0, a1, a2):
    lane = lax.broadcasted_iota(jnp.int32, a1.shape, 1)
    low = lane < 64
    near = pltpu.roll(jnp.where(low, a0, a2), 64, 1)
    far = jnp.where(low, pltpu.roll(a0, 65, 1), pltpu.roll(a2, 63, 1))
    return a1 + near + jnp.where((lane == 0) | (lane == 127), 0.0, far)


def conv(grid, mats, s, j):
    parts = [dot(mats[g], taps(grid, s, j, g)) for g in range(4)]
    result = []
    for x in range(2):
        sides = []
        for yy in range(2):
            a = [
                jnp.concatenate(
                    [p[48 * x + 16 * e : 48 * x + 16 * e + 16, 128 * yy : 128 * yy + 128] for p in parts],
                    axis=0,
                )
                for e in range(3)
            ]
            sides.append(shifted_sum(*a))
        result.append(jnp.concatenate(sides, axis=1))
    return result


def kernel(
    raw, cot, taps_in, pin_t, pout, down_in,
    coarse, grad_out, grad_in, grad_po, grad_down, dw_out,
    pin, pout_t, w2t, wide,
    fg, dg, gm, gdn, red, mats, mats_t, wacc, dwacc, points, swap, pair, rs, gyb, tot,
    f_send, f_recv, d_send, d_recv, c_send, c_recv, r_send, r_recv,
    rs_send, rs_recv, gy_send, gy_recv, ag_send, ag_recv, pair_send, pair_recv, own_sem,
):
    ix, iy = lax.axis_index("gx"), lax.axis_index("gy")
    mx, my = ix % 4, iy % 2
    mine = mx * 2 + my
    bx, by = ix - mx, iy - my

    for grid in (fg, dg):
        for cond, at in ((ix == 0, 0), (ix == NGX - 1, 3)):

            @pl.when(cond)
            def _(grid=grid, at=at):
                @pl.loop(0, S)
                def _(s):
                    grid[s, at] = jnp.zeros((10, C, 128), BF16)

        for cond, at in ((iy == 0, 0), (iy == NGY - 1, 9)):

            @pl.when(cond)
            def _(grid=grid, at=at):
                @pl.loop(0, S)
                def _(s):
                    grid[s, :, at] = jnp.zeros((4, C, 128), BF16)

    barrier = pltpu.get_barrier_semaphore()
    core, chip = ix % 2, ix // 2
    peers = [((ix + k) % NGX, iy) for k in range(2, NGX, 2)]
    peers += [(ix + 1 - 2 * core, iy), ((ix + NGX - 1 + 2 * core) % NGX, iy)]
    peers += [(ix, (iy + k) % NGY) for k in range(1, NGY)]
    peers += [((ix + p) % NGX, (iy + q) % NGY) for p in (1, NGX - 1) for q in (1, NGY - 1)]
    peers += [(bx + (mine + k) % 8 // 2, by + (mine + k) % 2) for k in range(1, 8)]
    for peer in peers:
        pl.semaphore_signal(barrier, inc=1, device_id=peer, device_id_type=MESH)

    def remote(src, dst, send, recv, to):
        return pltpu.make_async_remote_copy(
            src_ref=src, dst_ref=dst, send_sem=send, recv_sem=recv, device_id=to, device_id_type=MESH
        )

    def cot_copy(k):
        to = (mine + k) % 8
        tx, ty = to // 2, to % 2
        return remote(
            cot.at[tx, pl.ds(ty * 4, 4)], gdn.at[mine], c_send.at[to], c_recv.at[mine], (bx + tx, by + ty)
        )

    def cot_arrival(s):
        return remote(cot.at[0, pl.ds(0, 4)], gdn.at[s], c_send.at[s], c_recv.at[s], (ix, iy))

    def send_cot():
        for k in range(1, 8):
            cot_copy(k).start()

    gdn[mine] = cot[mx, pl.ds(my * 4, 4)]

    pin[...] = pin_t[...].astype(F32).T.astype(BF16)
    pout_t[...] = pout[...].astype(F32).T.astype(BF16)
    wide[...] = down_in[...].astype(F32)
    for k in range(8):
        at = 64 * (k // 2)
        w2t[at : at + 64, k % 2 * 128 : k % 2 * 128 + 128] = wide[pl.ds(k, 64, stride=8), :].astype(BF16)

    row = lax.broadcasted_iota(jnp.int32, (16, 192), 0)
    col = lax.broadcasted_iota(jnp.int32, (16, 192), 1)
    diag = row == col % 16
    tap = lax.broadcasted_iota(jnp.int32, (27, 192), 0)
    spot = lax.broadcasted_iota(jnp.int32, (27, 192), 1)
    flat = taps_in[...].astype(F32)
    coefficients = jnp.concatenate([flat[a, b] for a in range(3) for b in range(3)], axis=0).astype(BF16)
    for q in range(6):
        x, e = q // 3, q % 3
        a = spot // 48 - x
        at = 9 * a + 3 * (spot // 16 % 3) + e
        inside = (a >= 0) & (a <= 2)
        for to, place in ((mats, at), (mats_t, 26 - at)):
            spread = dot(coefficients, ((tap == place) & inside).astype(BF16), TN)
            for g in range(4):
                to[g, 16 * q : 16 * q + 16] = jnp.where(diag, spread[16 * g : 16 * g + 16], 0.0).astype(BF16)
    wacc[...] = jnp.zeros_like(wacc)
    dwacc[...] = jnp.zeros_like(dwacc)
    points[...] = jnp.zeros_like(points)

    zi = lax.broadcasted_iota(jnp.int32, (128, 128), 0)
    li = lax.broadcasted_iota(jnp.int32, (128, 128), 1)
    perm = (zi == jnp.where(li < 64, 2 * li, 2 * li - 127)).astype(BF16)

    def rims(grid, s, send, recv):
        whole, inner = pl.ds(1, 8), pl.ds(1, 2)
        west, east, south, north = ix > 0, ix < NGX - 1, iy > 0, iy < NGY - 1
        listed = [
            (west, east, (ix - 1, iy), (1, whole), (3, whole)),
            (east, west, (ix + 1, iy), (2, whole), (0, whole)),
            (south, north, (ix, iy - 1), (inner, 1), (inner, 9)),
            (north, south, (ix, iy + 1), (inner, 8), (inner, 0)),
            (west & south, east & north, (ix - 1, iy - 1), (1, 1), (3, 9)),
            (west & north, east & south, (ix - 1, iy + 1), (1, 8), (3, 0)),
            (east & south, west & north, (ix + 1, iy - 1), (2, 1), (0, 9)),
            (east & north, west & south, (ix + 1, iy + 1), (2, 8), (0, 0)),
        ]
        return [
            (goes, comes, remote(grid.at[(s, *src)], grid.at[(s, *dst)], send.at[s, d], recv.at[s, d], to))
            for d, (goes, comes, to, src, dst) in enumerate(listed)
        ]

    def send_rims(grid, s, send, recv):
        for goes, _, copy in rims(grid, s, send, recv):
            pl.when(goes)(copy.start)

    def await_rims(grid, s, send, recv):
        for _, comes, copy in rims(grid, s, send, recv):
            pl.when(comes)(copy.wait_recv)

    def prepare(s):
        for h in range(4):
            block = raw[s, 16 * h : 16 * h + 16].reshape(256, 128)
            turned = dot(block, perm).reshape(16, 16, 128)
            turned = jnp.swapaxes(turned, 0, 1).astype(BF16)
            for x in range(2):
                fg[s, 1 + x, 1:9, 16 * h : 16 * h + 16, :] = turned[8 * x : 8 * x + 8]

    def coarse_copy(s):
        return remote(
            red.at[s], coarse.at[mx, pl.ds(my * 4, 4)], r_send.at[s], r_recv.at[mine], (bx + s // 2, by + s % 2)
        )

    def coarse_arrival(s):
        return remote(
            red.at[s], coarse.at[s // 2, pl.ds(s % 2 * 4, 4)], r_send.at[s], r_recv.at[s], (ix, iy)
        )

    def own_coarse():
        return pltpu.make_async_copy(red.at[mine], coarse.at[mx, pl.ds(my * 4, 4)], own_sem)

    for s in range(2):
        prepare(s)
    pl.semaphore_wait(barrier, len(peers))
    pl.when(mine < 2)(send_cot)
    for s in range(2):
        send_rims(fg, s, f_send, f_recv)

    @pl.loop(0, S)
    def _(s):
        @pl.when(s < S - 2)
        def _():
            prepare(s + 2)
            pl.when(mine == s + 2)(send_cot)
            send_rims(fg, s + 2, f_send, f_recv)

        await_rims(fg, s, f_send, f_recv)

        @pl.when(s != mine)
        def _():
            cot_arrival(s).wait_recv()

        @pl.loop(0, 4, unroll=2)
        def _(j):
            down = gdn[s, j]
            none = jnp.zeros_like(down)
            down = jnp.concatenate(
                [jnp.concatenate([down, none], axis=1), jnp.concatenate([none, down], axis=1)], axis=0
            )
            gm_all = dot(w2t[...], down, NT).astype(BF16)
            depth = conv(fg, mats, s, j)
            stacked, lefts = [], []
            for x in range(2):
                dep = depth[x].astype(BF16)
                gm_x = jnp.concatenate(
                    [gm_all[128 * x : 128 * x + 64], gm_all[128 * x + 64 : 128 * x + 128]], axis=1
                )
                pre_x, grad_x = dot(pin[...], dep), dot(pout_t[...], gm_x)
                acts, gpres = [], []
                for h in range(0, HID, 64):
                    pre, grad = pre_x[h : h + 64], grad_x[h : h + 64]
                    sq = pre * pre
                    t = jnp.tanh(pre * (G0 + G1 * sq))
                    up = 0.5 + 0.5 * t
                    acts.append((pre * up).astype(BF16))
                    slope = up + 0.5 * pre * (1.0 - t * t) * (G0 + 3 * G1 * sq)
                    gpres.append((grad * slope).astype(BF16))
                act, gpre = jnp.concatenate(acts, axis=0), jnp.concatenate(gpres, axis=0)
                own = jnp.concatenate(
                    [fg[s, 1 + x, 1 + 2 * j + yy].astype(F32) for yy in range(2)], axis=1
                )
                merged = (own + dot(pout[...], act)).astype(BF16)
                stacked += [merged[:, :128], merged[:, 128:]]
                points[0] += dot(act, gm_x, NT)
                points[1] += dot(gpre, dep, NT)
                gdep = dot(pin_t[...], gpre).astype(BF16)
                sides = []
                for yy in range(2):
                    part = gdep[:, 128 * yy : 128 * yy + 128]
                    dg[s, 1 + x, 1 + 2 * j + yy] = part
                    gm[s, x, 2 * j + yy] = gm_x[:, 128 * yy : 128 * yy + 128]
                    here = part.astype(F32)
                    none = jnp.zeros_like(here)
                    sides.append((shifted_sum(none, none, here), here, shifted_sum(here, none, none)))
                for e in range(3):
                    lefts.append(jnp.concatenate([sides[0][e], sides[1][e]], axis=1).astype(BF16))
            for g in range(4):
                left = jnp.concatenate([m[16 * g : 16 * g + 16] for m in lefts], axis=0)
                dwacc[g] += dot(left, taps(fg, s, j, g), NT)
            stacked = jnp.concatenate(stacked, axis=0)
            term = dot(stacked, down)
            wacc[256:512] += term[:, :128]
            wacc[512:768] += term[:, 128:]
            both = dot(stacked, w2t[...], TN)
            red[s, j] = (both[:64, :128] + both[64:, 128:]).astype(BF16)

        send_rims(dg, s, d_send, d_recv)

        @pl.when(s != mine)
        def _():
            coarse_copy(s).start()

    own_coarse().start()

    spot = lax.broadcasted_iota(jnp.int32, (192, 128), 0)
    tap = lax.broadcasted_iota(jnp.int32, (192, 128), 1)
    found = jnp.zeros((C, 128), F32)
    for q in range(6):
        a = spot // 48 - q // 3
        picks = (tap == 9 * a + 3 * (spot // 16 % 3) + q % 3) & (a >= 0) & (a <= 2)
        block = jnp.concatenate(
            [jnp.where(diag, dwacc[g, 16 * q : 16 * q + 16, :], 0.0) for g in range(4)], axis=0
        )
        found += lax.dot_general(
            block, picks.astype(F32), NN, precision=lax.Precision.HIGHEST, preferred_element_type=F32
        )
    wacc[768:832] = found
    wacc[0:256] = jnp.concatenate([points[0], points[1]], axis=1)

    def block(start, rows):
        return pl.ds(pl.multiple_of(start, 8), rows)

    def other(k):
        return (chip + k) % 8

    def pair_copy():
        give = block((1 - core) * HALF, HALF)
        return remote(wacc.at[give], pair, pair_send.at[0], pair_recv.at[0], (ix + 1 - 2 * core, iy))

    def rs_copy(k):
        give = block(core * HALF + other(k) * PART, PART)
        return remote(wacc.at[give], rs.at[chip], rs_send.at[k], rs_recv.at[8 - k], (2 * other(k) + core, iy))

    def rs_arrival(k):
        give = block(core * HALF, PART)
        return remote(wacc.at[give], rs.at[other(k)], rs_send.at[k], rs_recv.at[k], (ix, iy))

    def gy_copy(k):
        return remote(gyb.at[iy], gyb.at[iy], gy_send.at[k], gy_recv.at[NGY - k], (ix, (iy + k) % NGY))

    def gy_arrival(k):
        slot = (iy + k) % NGY
        return remote(gyb.at[slot], gyb.at[slot], gy_send.at[k], gy_recv.at[k], (ix, iy))

    def ag_copy(k):
        rows = block(core * HALF + chip * PART, PART)
        return remote(tot.at[rows], tot.at[rows], ag_send.at[k], ag_recv.at[8 - k], (2 * other(k) + core, iy))

    def ag_arrival(k):
        rows = block(core * HALF + other(k) * PART, PART)
        return remote(tot.at[rows], tot.at[rows], ag_send.at[k], ag_recv.at[k], (ix, iy))

    def last_copy():
        rows = block(core * HALF, HALF)
        return remote(tot.at[rows], tot.at[rows], pair_send.at[1], pair_recv.at[1], (ix + 1 - 2 * core, iy))

    def last_arrival():
        rows = block((1 - core) * HALF, HALF)
        return remote(tot.at[rows], tot.at[rows], pair_send.at[1], pair_recv.at[1], (ix, iy))

    def total(buffer):
        result = buffer[0]
        for q in range(1, 8):
            result = result + buffer[q]
        return result

    pair_copy().start()

    @pl.loop(0, S)
    def _(s):
        await_rims(dg, s, d_send, d_recv)

        @pl.loop(0, 4, unroll=2)
        def _(j):
            adjoint = conv(dg, mats_t, s, j)
            for x in range(2):
                for yy in range(2):
                    at = 2 * j + yy
                    summed = gm[s, x, at].astype(F32) + adjoint[x][:, 128 * yy : 128 * yy + 128]
                    back = dot(summed.astype(BF16), perm, NT)
                    swap[8 * x + at] = back

        for h in range(4):
            turned = jnp.swapaxes(swap[:, 16 * h : 16 * h + 16, :], 0, 1)
            grad_out[s, 16 * h : 16 * h + 16] = turned.astype(BF16)

        @pl.when(s == 0)
        def _():
            pair_copy().wait_recv()
            wacc[block(core * HALF, HALF)] += pair[...]
            for k in range(1, 8):
                rs_copy(k).start()

        @pl.when(s == 2)
        def _():
            rs[chip] = wacc[block(core * HALF + chip * PART, PART)]
            for k in range(1, 8):
                rs_arrival(k).wait_recv()
            gyb[iy] = total(rs)
            for k in range(1, NGY):
                gy_copy(k).start()

        @pl.when(s == 4)
        def _():
            for k in range(1, NGY):
                gy_arrival(k).wait_recv()
            tot[block(core * HALF + chip * PART, PART)] = total(gyb) * SCALE
            for k in range(1, 8):
                ag_copy(k).start()

        @pl.when(s == 6)
        def _():
            for k in range(1, 8):
                ag_arrival(k).wait_recv()
            last_copy().start()

    last_arrival().wait_recv()
    both = tot[0:256].T
    grad_po[...] = both[:64]
    grad_in[...] = both[64:]
    for k in range(8):
        at = 256 + 256 * (k % 2) + 64 * (k // 2)
        grad_down[pl.ds(k, 64, stride=8), :] = tot[at : at + 64]
    flat = tot[768:832].T
    for k in range(9):
        dw_out[k // 3, k % 3] = flat[3 * k : 3 * k + 3]

    own_coarse().wait()

    @pl.loop(0, S)
    def _(s):
        @pl.when(s != mine)
        def _():
            coarse_arrival(s).wait_recv()
            coarse_copy(s).wait_send()

        for grid, send, recv in ((fg, f_send, f_recv), (dg, d_send, d_recv)):
            for goes, _, copy in rims(grid, s, send, recv):
                pl.when(goes)(copy.wait_send)

    for k in range(1, 8):
        cot_copy(k).wait_send()
        rs_copy(k).wait_send()
        ag_copy(k).wait_send()
        gy_copy(k).wait_send()
    pair_copy().wait_send()
    last_copy().wait_send()


def hand_over(*refs):
    sems = refs[12]
    pairs = [(i, o) for n, (i, o) in enumerate(zip(refs[:6], refs[6:12])) if n != 1]
    pairs += [(refs[1].at[s], refs[7].at[s]) for s in range(S)]
    copies = [pltpu.make_async_copy(i, o, sems.at[n]) for n, (i, o) in enumerate(pairs)]
    for copy in copies:
        copy.start()
    for copy in copies:
        copy.wait()


def per_device(fields, depth_kernel, point_in, point_out, down_kernel, cotangent):
    raw = fields.reshape(S, C, 16, 128)
    cot = cotangent[0, 0, 0].transpose(1, 2, 3, 0)
    taps_in = depth_kernel.transpose(1, 2, 3, 0)
    down_in = down_kernel.transpose(1, 2, 3, 4, 0).reshape(8 * C, C2)
    vmem = pl.BlockSpec(memory_space=pltpu.VMEM)
    dma = pltpu.SemaphoreType.DMA
    hbm = pl.BlockSpec(memory_space=pl.ANY)
    results = pl.pallas_call(
        kernel,
        out_shape=(
            jax.ShapeDtypeStruct((4, 8, 64, 128), BF16),
            jax.ShapeDtypeStruct((S, C, 16, 128), BF16),
            jax.ShapeDtypeStruct((C, HID), F32),
            jax.ShapeDtypeStruct((C, HID), F32),
            jax.ShapeDtypeStruct((8 * C, C2), F32),
            jax.ShapeDtypeStruct((3, 3, 3, C), F32),
        ),
        in_specs=[vmem] * 6,
        out_specs=[vmem] * 6,
        scratch_shapes=[
            pltpu.VMEM((HID, C), BF16),
            pltpu.VMEM((HID, C), BF16),
            pltpu.VMEM((256, 256), BF16),
            pltpu.VMEM((8 * C, C2), F32),
            pltpu.VMEM((S, 4, 10, C, 128), BF16),
            pltpu.VMEM((S, 4, 10, C, 128), BF16),
            pltpu.VMEM((S, 2, 8, C, 128), BF16),
            pltpu.VMEM((S, 4, 64, 128), BF16),
            pltpu.VMEM((S, 4, 64, 128), BF16),
            pltpu.VMEM((4, 96, 192), BF16),
            pltpu.VMEM((4, 96, 192), BF16),
            pltpu.VMEM((2 * HALF, 128), F32),
            pltpu.VMEM((4, 96, 192), F32),
            pltpu.VMEM((2, 256, 64), F32),
            pltpu.VMEM((16, C, 128), F32),
            pltpu.VMEM((HALF, 128), F32),
            pltpu.VMEM((8, PART, 128), F32),
            pltpu.VMEM((NGY, PART, 128), F32),
            pltpu.VMEM((2 * HALF, 128), F32),
            dma((S, 8)), dma((S, 8)), dma((S, 8)), dma((S, 8)),
            dma((8,)), dma((8,)), dma((8,)), dma((8,)),
            dma((8,)), dma((8,)), dma((NGY,)), dma((NGY,)), dma((8,)), dma((8,)), dma((2,)), dma((2,)),
            dma,
        ],
        compiler_params=pltpu.CompilerParams(
            collective_id=0, has_side_effects=True, vmem_limit_bytes=36 * 2**20
        ),
    )(raw, cot, taps_in, point_in.T, point_out, down_in)
    coarse, grad, grad_in, grad_po, grad_down, dw = pl.pallas_call(
        hand_over,
        out_shape=[jax.ShapeDtypeStruct(r.shape, r.dtype) for r in results],
        in_specs=[hbm] * 6,
        out_specs=[hbm] * 6,
        scratch_shapes=[dma((S + 5,))],
        compiler_params=pltpu.CompilerParams(vmem_limit_bytes=2**20),
        cost_estimate=pl.CostEstimate(flops=0, bytes_accessed=2**23, transcendentals=0),
    )(*results)
    coarse = coarse.transpose(3, 0, 1, 2)[None, None, None]
    grad_down = grad_down.reshape(C, 2, 2, 2, C2).transpose(4, 0, 1, 2, 3)
    dw = dw.transpose(3, 0, 1, 2)
    return coarse, grad.reshape(fields.shape), dw, grad_in.T, grad_po, grad_down


def solution(mesh):
    split = P("gx", "gy", None, None, None, None, None)
    fine = P(None, None, "gx", "gy", None)
    return jax.shard_map(
        per_device,
        mesh=mesh,
        in_specs=(fine, P(), P(), P(), P(), split),
        out_specs=(split, fine, P(), P(), P(), P()),
        check_vma=False,
    )
```

```python
import math

import jax
import jax.numpy as jnp
from jax import lax
from jax.experimental import pallas as pl
from jax.experimental.pallas import tpu as pltpu
from jax.sharding import PartitionSpec as P

NGX, NGY = 16, 8
S, C, HID, C2 = 8, 64, 256, 128
F32, BF16 = jnp.float32, jnp.bfloat16
MESH = pl.DeviceIdType.MESH
NN = (((1,), (0,)), ((), ()))
NT = (((1,), (1,)), ((), ()))
TN = (((0,), (0,)), ((), ()))
G0 = math.sqrt(2.0 / math.pi)
G1 = G0 * 0.044715
HALF, PART = 448, 56
SCALE = 1.0 / math.sqrt(8 * 32 * 64 * 128)


def dot(a, b, dims=NN):
    return lax.dot_general(a, b, dims, preferred_element_type=F32)


def taps(grid, s, j, g):
    sides = []
    for yy in range(2):
        block = grid[s, :, pl.ds(2 * j + yy, 3), 16 * g : 16 * g + 16, :]
        sides.append(block.reshape(192, 128))
    return jnp.concatenate(sides, axis=1)


def shifted_sum(a0, a1, a2):
    lane = lax.broadcasted_iota(jnp.int32, a1.shape, 1)
    low = lane < 64
    near = pltpu.roll(jnp.where(low, a0, a2), 64, 1)
    far = jnp.where(low, pltpu.roll(a0, 65, 1), pltpu.roll(a2, 63, 1))
    return a1 + near + jnp.where((lane == 0) | (lane == 127), 0.0, far)


def conv(grid, mats, s, j):
    parts = [dot(mats[g], taps(grid, s, j, g)) for g in range(4)]
    result = []
    for x in range(2):
        sides = []
        for yy in range(2):
            a = [
                jnp.concatenate(
                    [p[48 * x + 16 * e : 48 * x + 16 * e + 16, 128 * yy : 128 * yy + 128] for p in parts],
                    axis=0,
                )
                for e in range(3)
            ]
            sides.append(shifted_sum(*a))
        result.append(jnp.concatenate(sides, axis=1))
    return result


def kernel(
    raw_hbm, cot, taps_in, pin_t, pout, down_in,
    coarse, grad_hbm, grad_in, grad_po, grad_down, dw_out,
    raw, grad_out, pin, pout_t, w2t, wide,
    fg, dg, gm, mg, gdn, red, mats, mats_t, wacc, dwacc, points, swap, pair, rs, gyb, tot, flat,
    f_send, f_recv, d_send, d_recv, c_send, c_recv, r_send, r_recv,
    rs_send, rs_recv, gy_send, gy_recv, ag_send, ag_recv, pair_send, pair_recv, own_sem, in_sem, out_sem,
):
    ix, iy = lax.axis_index("gx"), lax.axis_index("gy")
    mx, my = ix % 4, iy % 2
    mine = mx * 2 + my
    bx, by = ix - mx, iy - my

    barrier = pltpu.get_barrier_semaphore()
    core, chip = ix % 2, ix // 2
    peers = [((ix + k) % NGX, iy) for k in range(2, NGX, 2)]
    peers += [(ix + 1 - 2 * core, iy), ((ix + NGX - 1 + 2 * core) % NGX, iy)]
    peers += [(ix, (iy + k) % NGY) for k in range(1, NGY)]
    peers += [((ix + p) % NGX, (iy + q) % NGY) for p in (1, NGX - 1) for q in (1, NGY - 1)]
    peers += [(bx + (mine + k) % 8 // 2, by + (mine + k) % 2) for k in range(1, 8)]
    for peer in peers:
        pl.semaphore_signal(barrier, inc=1, device_id=peer, device_id_type=MESH)

    def load(s):
        return pltpu.make_async_copy(raw_hbm.at[s], raw.at[s], in_sem.at[s])

    def store(s):
        return pltpu.make_async_copy(grad_out.at[s], grad_hbm.at[s], out_sem.at[s])

    for s in range(S):
        load(s).start()

    for grid in (fg, dg):
        for cond, at in ((ix == 0, 0), (ix == NGX - 1, 3)):

            @pl.when(cond)
            def _(grid=grid, at=at):
                @pl.loop(0, S)
                def _(s):
                    grid[s, at] = jnp.zeros((10, C, 128), BF16)

        for cond, at in ((iy == 0, 0), (iy == NGY - 1, 9)):

            @pl.when(cond)
            def _(grid=grid, at=at):
                @pl.loop(0, S)
                def _(s):
                    grid[s, :, at] = jnp.zeros((4, C, 128), BF16)

    def remote(src, dst, send, recv, to):
        return pltpu.make_async_remote_copy(
            src_ref=src, dst_ref=dst, send_sem=send, recv_sem=recv, device_id=to, device_id_type=MESH
        )

    def cot_copy(k):
        to = (mine + k) % 8
        tx, ty = to // 2, to % 2
        return remote(
            cot.at[tx, pl.ds(ty * 4, 4)], gdn.at[mine], c_send.at[to], c_recv.at[mine], (bx + tx, by + ty)
        )

    def cot_arrival(s):
        return remote(cot.at[0, pl.ds(0, 4)], gdn.at[s], c_send.at[s], c_recv.at[s], (ix, iy))

    def send_cot():
        for k in range(1, 8):
            cot_copy(k).start()

    def own_cot():
        return pltpu.make_async_copy(cot.at[mx, pl.ds(my * 4, 4)], gdn.at[mine], own_sem.at[1])

    own_cot().start()

    zi = lax.broadcasted_iota(jnp.int32, (128, 128), 0)
    li = lax.broadcasted_iota(jnp.int32, (128, 128), 1)
    perm = (zi == jnp.where(li < 64, 2 * li, 2 * li - 127)).astype(BF16)
    unperm = (li == jnp.where(zi < 64, 2 * zi, 2 * zi - 127)).astype(BF16)

    def rims(grid, s, send, recv):
        whole, inner = pl.ds(1, 8), pl.ds(1, 2)
        west, east, south, north = ix > 0, ix < NGX - 1, iy > 0, iy < NGY - 1
        listed = [
            (west, east, (ix - 1, iy), (1, whole), (3, whole)),
            (east, west, (ix + 1, iy), (2, whole), (0, whole)),
            (south, north, (ix, iy - 1), (inner, 1), (inner, 9)),
            (north, south, (ix, iy + 1), (inner, 8), (inner, 0)),
            (west & south, east & north, (ix - 1, iy - 1), (1, 1), (3, 9)),
            (west & north, east & south, (ix - 1, iy + 1), (1, 8), (3, 0)),
            (east & south, west & north, (ix + 1, iy - 1), (2, 1), (0, 9)),
            (east & north, west & south, (ix + 1, iy + 1), (2, 8), (0, 0)),
        ]
        return [
            (goes, comes, remote(grid.at[(s, *src)], grid.at[(s, *dst)], send.at[s, d], recv.at[s, d], to))
            for d, (goes, comes, to, src, dst) in enumerate(listed)
        ]

    def send_rims(grid, s, send, recv):
        for goes, _, copy in rims(grid, s, send, recv):
            pl.when(goes)(copy.start)

    def await_rims(grid, s, send, recv):
        for _, comes, copy in rims(grid, s, send, recv):
            pl.when(comes)(copy.wait_recv)

    def prepare(s):
        load(s).wait()
        for h in range(4):
            block = raw[s, 16 * h : 16 * h + 16].reshape(256, 128)
            turned = dot(block, perm).reshape(16, 16, 128)
            turned = jnp.swapaxes(turned, 0, 1).astype(BF16)
            for x in range(2):
                fg[s, 1 + x, 1:9, 16 * h : 16 * h + 16, :] = turned[8 * x : 8 * x + 8]

    def coarse_copy(s):
        return remote(
            red.at[s], coarse.at[mx, pl.ds(my * 4, 4)], r_send.at[s], r_recv.at[mine], (bx + s // 2, by + s % 2)
        )

    def coarse_arrival(s):
        return remote(
            red.at[s], coarse.at[s // 2, pl.ds(s % 2 * 4, 4)], r_send.at[s], r_recv.at[s], (ix, iy)
        )

    def own_coarse():
        return pltpu.make_async_copy(red.at[mine], coarse.at[mx, pl.ds(my * 4, 4)], own_sem.at[0])

    for s in range(2):
        prepare(s)
    pl.semaphore_wait(barrier, len(peers))
    pl.when(mine < 2)(send_cot)
    for s in range(2):
        send_rims(fg, s, f_send, f_recv)

    pin[...] = pin_t[...].astype(F32).T.astype(BF16)
    pout_t[...] = pout[...].astype(F32).T.astype(BF16)
    wide[...] = down_in[...].astype(F32)
    for k in range(8):
        at = 64 * (k // 2)
        w2t[at : at + 64, k % 2 * 128 : k % 2 * 128 + 128] = wide[pl.ds(k, 64, stride=8), :].astype(BF16)

    row = lax.broadcasted_iota(jnp.int32, (16, 192), 0)
    col = lax.broadcasted_iota(jnp.int32, (16, 192), 1)
    diag = row == col % 16
    tap = lax.broadcasted_iota(jnp.int32, (27, 192), 0)
    spot = lax.broadcasted_iota(jnp.int32, (27, 192), 1)
    given = taps_in[...].astype(F32)
    coefficients = jnp.concatenate([given[a, b] for a in range(3) for b in range(3)], axis=0).astype(BF16)
    for q in range(6):
        x, e = q // 3, q % 3
        a = spot // 48 - x
        at = 9 * a + 3 * (spot // 16 % 3) + e
        inside = (a >= 0) & (a <= 2)
        for to, place in ((mats, at), (mats_t, 26 - at)):
            spread = dot(coefficients, ((tap == place) & inside).astype(BF16), TN)
            for g in range(4):
                to[g, 16 * q : 16 * q + 16] = jnp.where(diag, spread[16 * g : 16 * g + 16], 0.0).astype(BF16)
    wacc[...] = jnp.zeros_like(wacc)
    dwacc[...] = jnp.zeros_like(dwacc)
    points[...] = jnp.zeros_like(points)

    @pl.loop(0, S)
    def _(s):
        @pl.when(s < S - 2)
        def _():
            prepare(s + 2)
            pl.when(mine == s + 2)(send_cot)
            send_rims(fg, s + 2, f_send, f_recv)

        await_rims(fg, s, f_send, f_recv)

        @pl.when(s != mine)
        def _():
            cot_arrival(s).wait_recv()

        @pl.when(s == mine)
        def _():
            own_cot().wait()

        @pl.loop(0, 2)
        def _(pair_of):
            downs = []
            for jj in range(2):
                down = gdn[s, 2 * pair_of + jj]
                none = jnp.zeros_like(down)
                downs += [jnp.concatenate([down, none], axis=1), jnp.concatenate([none, down], axis=1)]
            downs = jnp.concatenate(downs, axis=0)
            gm_all = dot(w2t[...], downs, NT).astype(BF16)
            pools = ([], [], [], [])
            stacks = []
            lefts = [[], [], [], [], [], []]
            for jj in range(2):
                j = 2 * pair_of + jj
                gm_j = gm_all[:, 128 * jj : 128 * jj + 128]
                depth = conv(fg, mats, s, j)
                stacked = []
                for x in range(2):
                    dep = depth[x].astype(BF16)
                    gm_x = jnp.concatenate(
                        [gm_j[128 * x : 128 * x + 64], gm_j[128 * x + 64 : 128 * x + 128]], axis=1
                    )
                    pre_x, grad_x = dot(pin[...], dep), dot(pout_t[...], gm_x)
                    acts, gpres = [], []
                    for h in range(0, HID, 64):
                        pre, grad = pre_x[h : h + 64], grad_x[h : h + 64]
                        sq = pre * pre
                        t = jnp.tanh(pre * (G0 + G1 * sq))
                        up = 0.5 + 0.5 * t
                        acts.append((pre * up).astype(BF16))
                        slope = up + 0.5 * pre * (1.0 - t * t) * (G0 + 3 * G1 * sq)
                        gpres.append((grad * slope).astype(BF16))
                    act, gpre = jnp.concatenate(acts, axis=0), jnp.concatenate(gpres, axis=0)
                    own = jnp.concatenate(
                        [fg[s, 1 + x, 1 + 2 * j + yy].astype(F32) for yy in range(2)], axis=1
                    )
                    merged = (own + dot(pout[...], act)).astype(BF16)
                    stacked += [merged[:, :128], merged[:, 128:]]
                    for pool, part in zip(pools, (act, gm_x, gpre, dep)):
                        pool.append(part)
                    gdep = dot(pin_t[...], gpre).astype(BF16)
                    for yy in range(2):
                        part = gdep[:, 128 * yy : 128 * yy + 128]
                        dg[s, 1 + x, 1 + 2 * j + yy] = part
                        gm[s, x, 2 * j + yy] = gm_x[:, 128 * yy : 128 * yy + 128]
                        here = part.astype(F32)
                        none = jnp.zeros_like(here)
                        lefts[3 * x].append(shifted_sum(none, none, here).astype(BF16))
                        lefts[3 * x + 1].append(part)
                        lefts[3 * x + 2].append(shifted_sum(here, none, none).astype(BF16))
                stacked = jnp.concatenate(stacked, axis=0)
                mg[s, j] = stacked
                stacks.append(stacked)
            act, gm_x, gpre, dep = (jnp.concatenate(pool, axis=1) for pool in pools)
            points[0] += dot(act, gm_x, NT)
            points[1] += dot(gpre, dep, NT)
            term = dot(jnp.concatenate(stacks, axis=1), downs)
            wacc[256:512] += term[:, :128]
            wacc[512:768] += term[:, 128:]
            lines = [jnp.concatenate(line, axis=1) for line in lefts]
            for g in range(4):
                left = jnp.concatenate([m[16 * g : 16 * g + 16] for m in lines], axis=0)
                right = [taps(fg, s, 2 * pair_of + jj, g) for jj in range(2)]
                dwacc[g] += dot(left, jnp.concatenate(right, axis=1), NT)

        send_rims(dg, s, d_send, d_recv)

    spot = lax.broadcasted_iota(jnp.int32, (192, 128), 0)
    tap = lax.broadcasted_iota(jnp.int32, (192, 128), 1)
    found = jnp.zeros((C, 128), F32)
    for q in range(6):
        a = spot // 48 - q // 3
        picks = (tap == 9 * a + 3 * (spot // 16 % 3) + q % 3) & (a >= 0) & (a <= 2)
        block = jnp.concatenate(
            [jnp.where(diag, dwacc[g, 16 * q : 16 * q + 16, :], 0.0) for g in range(4)], axis=0
        )
        found += lax.dot_general(
            block, picks.astype(F32), NN, precision=lax.Precision.HIGHEST, preferred_element_type=F32
        )
    wacc[768:832] = found
    wacc[0:256] = jnp.concatenate([points[0], points[1]], axis=1)

    def block(start, rows):
        return pl.ds(pl.multiple_of(start, 8), rows)

    def other(k):
        return (chip + k) % 8

    def pair_copy():
        give = block((1 - core) * HALF, HALF)
        return remote(wacc.at[give], pair, pair_send.at[0], pair_recv.at[0], (ix + 1 - 2 * core, iy))

    def rs_copy(k):
        give = block(core * HALF + other(k) * PART, PART)
        return remote(wacc.at[give], rs.at[chip], rs_send.at[k], rs_recv.at[8 - k], (2 * other(k) + core, iy))

    def rs_arrival(k):
        give = block(core * HALF, PART)
        return remote(wacc.at[give], rs.at[other(k)], rs_send.at[k], rs_recv.at[k], (ix, iy))

    def gy_copy(k):
        return remote(gyb.at[iy], gyb.at[iy], gy_send.at[k], gy_recv.at[NGY - k], (ix, (iy + k) % NGY))

    def gy_arrival(k):
        slot = (iy + k) % NGY
        return remote(gyb.at[slot], gyb.at[slot], gy_send.at[k], gy_recv.at[k], (ix, iy))

    def ag_copy(k):
        slot = core * 8 + chip
        return remote(tot.at[slot], tot.at[slot], ag_send.at[k], ag_recv.at[8 - k], (2 * other(k) + core, iy))

    def ag_arrival(k):
        slot = core * 8 + other(k)
        return remote(tot.at[slot], tot.at[slot], ag_send.at[k], ag_recv.at[k], (ix, iy))

    def last_copy():
        rows = pl.ds(core * 8, 8)
        return remote(tot.at[rows], tot.at[rows], pair_send.at[1], pair_recv.at[1], (ix + 1 - 2 * core, iy))

    def last_arrival():
        rows = pl.ds(8 - core * 8, 8)
        return remote(tot.at[rows], tot.at[rows], pair_send.at[1], pair_recv.at[1], (ix, iy))

    def total(buffer):
        result = buffer[0]
        for q in range(1, 8):
            result = result + buffer[q]
        return result

    pair_copy().start()

    def reduce(s):
        rows = jnp.concatenate([mg[s, j] for j in range(4)], axis=1)
        both = dot(rows, w2t[...], TN)
        for j in range(4):
            at = 128 * j
            red[s, j] = (both[at : at + 64, :128] + both[at + 64 : at + 128, 128:]).astype(BF16)

    def send_coarse(s):
        @pl.when(s != mine)
        def _():
            coarse_copy(s).start()

        @pl.when(s == mine)
        def _():
            own_coarse().start()

    for s in range(2):
        reduce(s)
    pair_copy().wait_recv()
    wacc[block(core * HALF, HALF)] += pair[...]
    for k in range(1, 8):
        rs_copy(k).start()
    for s in range(2):
        send_coarse(s)

    @pl.loop(0, S)
    def _(s):
        await_rims(dg, s, d_send, d_recv)

        @pl.loop(0, 4, unroll=2)
        def _(j):
            adjoint = conv(dg, mats_t, s, j)
            sides = []
            for x in range(2):
                for yy in range(2):
                    summed = gm[s, x, 2 * j + yy].astype(F32) + adjoint[x][:, 128 * yy : 128 * yy + 128]
                    sides.append(summed.astype(BF16))
            back = dot(jnp.concatenate(sides, axis=0), unperm)
            for x in range(2):
                for yy in range(2):
                    at = 128 * x + 64 * yy
                    swap[8 * x + 2 * j + yy] = back[at : at + 64]

        for h in range(4):
            turned = jnp.swapaxes(swap[:, 16 * h : 16 * h + 16, :], 0, 1)
            grad_out[s, 16 * h : 16 * h + 16] = turned.astype(BF16)
        store(s).start()

        @pl.when(s < 3)
        def _():
            for k in range(2):
                reduce(2 + 2 * s + k)
                send_coarse(2 + 2 * s + k)

        @pl.when(s == 2)
        def _():
            rs[chip] = wacc[block(core * HALF + chip * PART, PART)]
            for k in range(1, 8):
                rs_arrival(k).wait_recv()
            gyb[iy] = total(rs)
            for k in range(1, NGY):
                gy_copy(k).start()

        @pl.when(s == 4)
        def _():
            for k in range(1, NGY):
                gy_arrival(k).wait_recv()
            tot[core * 8 + chip] = (total(gyb) * SCALE).astype(BF16)
            for k in range(1, 8):
                ag_copy(k).start()

        @pl.when(s == 6)
        def _():
            for k in range(1, 8):
                ag_arrival(k).wait_recv()
            last_copy().start()

    last_arrival().wait_recv()
    for slot in range(16):
        flat[PART * slot : PART * slot + PART] = tot[slot].astype(F32)
    both = flat[0:256].T
    grad_po[...] = both[:64]
    grad_in[...] = both[64:]
    for k in range(8):
        at = 256 + 256 * (k % 2) + 64 * (k // 2)
        grad_down[pl.ds(k, 64, stride=8), :] = flat[at : at + 64]
    lines = flat[768:832].T
    for k in range(9):
        dw_out[k // 3, k % 3] = lines[3 * k : 3 * k + 3]

    own_coarse().wait()

    @pl.loop(0, S)
    def _(s):
        @pl.when(s != mine)
        def _():
            coarse_arrival(s).wait_recv()
            coarse_copy(s).wait_send()

        store(s).wait()
        for grid, send, recv in ((fg, f_send, f_recv), (dg, d_send, d_recv)):
            for goes, _, copy in rims(grid, s, send, recv):
                pl.when(goes)(copy.wait_send)

    for k in range(1, 8):
        cot_copy(k).wait_send()
        rs_copy(k).wait_send()
        ag_copy(k).wait_send()
        gy_copy(k).wait_send()
    pair_copy().wait_send()
    last_copy().wait_send()


def hand_over(*refs):
    held, arrive, leave = refs[12:18], refs[18], refs[19]
    trips = [(refs[1].at[s], held[1].at[s], refs[7].at[s]) for s in range(S)]
    trips += [(refs[n], held[n], refs[6 + n]) for n in (0, 2, 3, 4, 5)]
    into = [pltpu.make_async_copy(a, b, arrive.at[n]) for n, (a, b, _) in enumerate(trips)]
    out = [pltpu.make_async_copy(b, c, leave.at[n]) for n, (_, b, c) in enumerate(trips)]
    for copy in into:
        copy.start()
    for first, then in zip(into, out):
        first.wait()
        then.start()
    for copy in out:
        copy.wait()


def per_device(fields, depth_kernel, point_in, point_out, down_kernel, cotangent):
    raw = fields.reshape(S, C, 16, 128)
    cot = cotangent[0, 0, 0].transpose(1, 2, 3, 0)
    taps_in = depth_kernel.transpose(1, 2, 3, 0)
    down_in = down_kernel.transpose(1, 2, 3, 4, 0).reshape(8 * C, C2)
    vmem = pl.BlockSpec(memory_space=pltpu.VMEM)
    dma = pltpu.SemaphoreType.DMA
    hbm = pl.BlockSpec(memory_space=pl.ANY)
    results = pl.pallas_call(
        kernel,
        out_shape=(
            jax.ShapeDtypeStruct((4, 8, 64, 128), BF16),
            jax.ShapeDtypeStruct((S, C, 16, 128), BF16),
            jax.ShapeDtypeStruct((C, HID), F32),
            jax.ShapeDtypeStruct((C, HID), F32),
            jax.ShapeDtypeStruct((8 * C, C2), F32),
            jax.ShapeDtypeStruct((3, 3, 3, C), F32),
        ),
        in_specs=[hbm] * 2 + [vmem] * 4,
        out_specs=[vmem, hbm] + [vmem] * 4,
        scratch_shapes=[
            pltpu.VMEM((S, C, 16, 128), BF16),
            pltpu.VMEM((S, C, 16, 128), BF16),
            pltpu.VMEM((HID, C), BF16),
            pltpu.VMEM((HID, C), BF16),
            pltpu.VMEM((256, 256), BF16),
            pltpu.VMEM((8 * C, C2), F32),
            pltpu.VMEM((S, 4, 10, C, 128), BF16),
            pltpu.VMEM((S, 4, 10, C, 128), BF16),
            pltpu.VMEM((S, 2, 8, C, 128), BF16),
            pltpu.VMEM((S, 4, 256, 128), BF16),
            pltpu.VMEM((S, 4, 64, 128), BF16),
            pltpu.VMEM((S, 4, 64, 128), BF16),
            pltpu.VMEM((4, 96, 192), BF16),
            pltpu.VMEM((4, 96, 192), BF16),
            pltpu.VMEM((2 * HALF, 128), F32),
            pltpu.VMEM((4, 96, 192), F32),
            pltpu.VMEM((2, 256, 64), F32),
            pltpu.VMEM((16, C, 128), F32),
            pltpu.VMEM((HALF, 128), F32),
            pltpu.VMEM((8, PART, 128), F32),
            pltpu.VMEM((NGY, PART, 128), F32),
            pltpu.VMEM((16, PART, 128), BF16),
            pltpu.VMEM((2 * HALF, 128), F32),
            dma((S, 8)), dma((S, 8)), dma((S, 8)), dma((S, 8)),
            dma((8,)), dma((8,)), dma((8,)), dma((8,)),
            dma((8,)), dma((8,)), dma((NGY,)), dma((NGY,)), dma((8,)), dma((8,)), dma((2,)), dma((2,)),
            dma((2,)), dma((S,)), dma((S,)),
        ],
        compiler_params=pltpu.CompilerParams(
            collective_id=0, has_side_effects=True, vmem_limit_bytes=56 * 2**20
        ),
    )(raw, cot, taps_in, point_in.T, point_out, down_in)
    coarse, grad, grad_in, grad_po, grad_down, dw = pl.pallas_call(
        hand_over,
        out_shape=[jax.ShapeDtypeStruct(r.shape, r.dtype) for r in results],
        in_specs=[hbm] * 6,
        out_specs=[hbm] * 6,
        scratch_shapes=[pltpu.VMEM(r.shape, r.dtype) for r in results] + [dma((S + 5,)), dma((S + 5,))],
        compiler_params=pltpu.CompilerParams(vmem_limit_bytes=56 * 2**20),
        cost_estimate=pl.CostEstimate(flops=0, bytes_accessed=2**23, transcendentals=0),
    )(*results)
    coarse = coarse.transpose(3, 0, 1, 2)[None, None, None]
    grad_down = grad_down.reshape(C, 2, 2, 2, C2).transpose(4, 0, 1, 2, 3)
    dw = dw.transpose(3, 0, 1, 2)
    return coarse, grad.reshape(fields.shape), dw, grad_in.T, grad_po, grad_down


def solution(mesh):
    split = P("gx", "gy", None, None, None, None, None)
    fine = P(None, None, "gx", "gy", None)
    return jax.shard_map(
        per_device,
        mesh=mesh,
        in_specs=(fine, P(), P(), P(), P(), split),
        out_specs=(split, fine, P(), P(), P(), P()),
        check_vma=False,
    )
```

```python
import math

import jax
import jax.numpy as jnp
from jax import lax
from jax.experimental import pallas as pl
from jax.experimental.pallas import tpu as pltpu
from jax.sharding import PartitionSpec as P

NGX, NGY = 16, 8
S, C, HID, C2 = 8, 64, 256, 128
F32, BF16 = jnp.float32, jnp.bfloat16
MESH = pl.DeviceIdType.MESH
NN = (((1,), (0,)), ((), ()))
NT = (((1,), (1,)), ((), ()))
TN = (((0,), (0,)), ((), ()))
G0 = math.sqrt(2.0 / math.pi)
G1 = G0 * 0.044715
HALF, PART = 448, 56
SCALE = 1.0 / math.sqrt(8 * 32 * 64 * 128)


def dot(a, b, dims=NN):
    return lax.dot_general(a, b, dims, preferred_element_type=F32)


def taps(grid, s, j, g):
    sides = []
    for yy in range(2):
        block = grid[s, :, pl.ds(2 * j + yy, 3), 16 * g : 16 * g + 16, :]
        sides.append(block.reshape(192, 128))
    return jnp.concatenate(sides, axis=1)


def shifted_sum(a0, a1, a2):
    lane = lax.broadcasted_iota(jnp.int32, a1.shape, 1)
    low = lane < 64
    near = pltpu.roll(jnp.where(low, a0, a2), 64, 1)
    far = jnp.where(low, pltpu.roll(a0, 65, 1), pltpu.roll(a2, 63, 1))
    return a1 + near + jnp.where((lane == 0) | (lane == 127), 0.0, far)


def conv(grid, mats, s, j):
    parts = [dot(mats[g], taps(grid, s, j, g)) for g in range(4)]
    result = []
    for x in range(2):
        sides = []
        for yy in range(2):
            a = [
                jnp.concatenate(
                    [p[48 * x + 16 * e : 48 * x + 16 * e + 16, 128 * yy : 128 * yy + 128] for p in parts],
                    axis=0,
                )
                for e in range(3)
            ]
            sides.append(shifted_sum(*a))
        result.append(jnp.concatenate(sides, axis=1))
    return result


def kernel(
    raw_hbm, cot, taps_in, pin_t, pout, down_in,
    coarse, grad_hbm, grad_in, grad_po, grad_down, dw_out,
    raw, grad_out, pin, pout_t, w2t, wide,
    fg, dg, gm, mg, gdn, red, mats, mats_t, wacc, dwacc, points, swap, pair, rs, gyb, tot, flat,
    f_send, f_recv, d_send, d_recv, c_send, c_recv, r_send, r_recv,
    rs_send, rs_recv, gy_send, gy_recv, ag_send, ag_recv, pair_send, pair_recv, own_sem, in_sem, out_sem,
):
    ix, iy = lax.axis_index("gx"), lax.axis_index("gy")
    mx, my = ix % 4, iy % 2
    mine = mx * 2 + my
    bx, by = ix - mx, iy - my

    barrier = pltpu.get_barrier_semaphore()
    core, chip = ix % 2, ix // 2
    peers = [((ix + k) % NGX, iy) for k in range(2, NGX, 2)]
    peers += [(ix + 1 - 2 * core, iy), ((ix + NGX - 1 + 2 * core) % NGX, iy)]
    peers += [(ix, (iy + k) % NGY) for k in range(1, NGY)]
    peers += [((ix + p) % NGX, (iy + q) % NGY) for p in (1, NGX - 1) for q in (1, NGY - 1)]
    peers += [(bx + (mine + k) % 8 // 2, by + (mine + k) % 2) for k in range(1, 8)]
    for peer in peers:
        pl.semaphore_signal(barrier, inc=1, device_id=peer, device_id_type=MESH)

    def load(s):
        return pltpu.make_async_copy(raw_hbm.at[s], raw.at[s], in_sem.at[s])

    def store(s):
        return pltpu.make_async_copy(grad_out.at[s], grad_hbm.at[s], out_sem.at[s])

    for s in range(S):
        load(s).start()

    for grid in (fg, dg):
        for cond, at in ((ix == 0, 0), (ix == NGX - 1, 3)):

            @pl.when(cond)
            def _(grid=grid, at=at):
                @pl.loop(0, S)
                def _(s):
                    grid[s, at] = jnp.zeros((10, C, 128), BF16)

        for cond, at in ((iy == 0, 0), (iy == NGY - 1, 9)):

            @pl.when(cond)
            def _(grid=grid, at=at):
                @pl.loop(0, S)
                def _(s):
                    grid[s, :, at] = jnp.zeros((4, C, 128), BF16)

    def remote(src, dst, send, recv, to):
        return pltpu.make_async_remote_copy(
            src_ref=src, dst_ref=dst, send_sem=send, recv_sem=recv, device_id=to, device_id_type=MESH
        )

    def cot_copy(k):
        to = (mine + k) % 8
        tx, ty = to // 2, to % 2
        return remote(
            cot.at[tx, pl.ds(ty * 4, 4)], gdn.at[mine], c_send.at[to], c_recv.at[mine], (bx + tx, by + ty)
        )

    def cot_arrival(s):
        return remote(cot.at[0, pl.ds(0, 4)], gdn.at[s], c_send.at[s], c_recv.at[s], (ix, iy))

    def send_cot():
        for k in range(1, 8):
            cot_copy(k).start()

    def own_cot():
        return pltpu.make_async_copy(cot.at[mx, pl.ds(my * 4, 4)], gdn.at[mine], own_sem.at[1])

    own_cot().start()

    zi = lax.broadcasted_iota(jnp.int32, (128, 128), 0)
    li = lax.broadcasted_iota(jnp.int32, (128, 128), 1)
    perm = (zi == jnp.where(li < 64, 2 * li, 2 * li - 127)).astype(BF16)
    unperm = (li == jnp.where(zi < 64, 2 * zi, 2 * zi - 127)).astype(BF16)

    def rims(grid, s, send, recv):
        whole, inner = pl.ds(1, 8), pl.ds(1, 2)
        west, east, south, north = ix > 0, ix < NGX - 1, iy > 0, iy < NGY - 1
        listed = [
            (west, east, (ix - 1, iy), (1, whole), (3, whole)),
            (east, west, (ix + 1, iy), (2, whole), (0, whole)),
            (south, north, (ix, iy - 1), (inner, 1), (inner, 9)),
            (north, south, (ix, iy + 1), (inner, 8), (inner, 0)),
            (west & south, east & north, (ix - 1, iy - 1), (1, 1), (3, 9)),
            (west & north, east & south, (ix - 1, iy + 1), (1, 8), (3, 0)),
            (east & south, west & north, (ix + 1, iy - 1), (2, 1), (0, 9)),
            (east & north, west & south, (ix + 1, iy + 1), (2, 8), (0, 0)),
        ]
        return [
            (goes, comes, remote(grid.at[(s, *src)], grid.at[(s, *dst)], send.at[s, d], recv.at[s, d], to))
            for d, (goes, comes, to, src, dst) in enumerate(listed)
        ]

    def send_rims(grid, s, send, recv):
        for goes, _, copy in rims(grid, s, send, recv):
            pl.when(goes)(copy.start)

    def await_rims(grid, s, send, recv):
        for _, comes, copy in rims(grid, s, send, recv):
            pl.when(comes)(copy.wait_recv)

    def prepare(s):
        load(s).wait()
        for h in range(4):
            block = raw[s, 16 * h : 16 * h + 16].reshape(256, 128)
            turned = dot(block, perm).reshape(16, 16, 128)
            turned = jnp.swapaxes(turned, 0, 1).astype(BF16)
            for x in range(2):
                fg[s, 1 + x, 1:9, 16 * h : 16 * h + 16, :] = turned[8 * x : 8 * x + 8]

    def coarse_copy(s):
        return remote(
            red.at[s], coarse.at[mx, pl.ds(my * 4, 4)], r_send.at[s], r_recv.at[mine], (bx + s // 2, by + s % 2)
        )

    def coarse_arrival(s):
        return remote(
            red.at[s], coarse.at[s // 2, pl.ds(s % 2 * 4, 4)], r_send.at[s], r_recv.at[s], (ix, iy)
        )

    def own_coarse():
        return pltpu.make_async_copy(red.at[mine], coarse.at[mx, pl.ds(my * 4, 4)], own_sem.at[0])

    for s in range(2):
        prepare(s)
    pl.semaphore_wait(barrier, len(peers))
    pl.when(mine < 2)(send_cot)
    for s in range(2):
        send_rims(fg, s, f_send, f_recv)

    pin[...] = pin_t[...].astype(F32).T.astype(BF16)
    pout_t[...] = pout[...].astype(F32).T.astype(BF16)
    wide[...] = down_in[...].astype(F32)
    for k in range(8):
        at = 64 * (k // 2)
        w2t[at : at + 64, k % 2 * 128 : k % 2 * 128 + 128] = wide[pl.ds(k, 64, stride=8), :].astype(BF16)

    row = lax.broadcasted_iota(jnp.int32, (16, 192), 0)
    col = lax.broadcasted_iota(jnp.int32, (16, 192), 1)
    diag = row == col % 16
    tap = lax.broadcasted_iota(jnp.int32, (27, 192), 0)
    spot = lax.broadcasted_iota(jnp.int32, (27, 192), 1)
    given = taps_in[...].astype(F32)
    coefficients = jnp.concatenate([given[a, b] for a in range(3) for b in range(3)], axis=0).astype(BF16)
    for q in range(6):
        x, e = q // 3, q % 3
        a = spot // 48 - x
        at = 9 * a + 3 * (spot // 16 % 3) + e
        inside = (a >= 0) & (a <= 2)
        for to, place in ((mats, at), (mats_t, 26 - at)):
            spread = dot(coefficients, ((tap == place) & inside).astype(BF16), TN)
            for g in range(4):
                to[g, 16 * q : 16 * q + 16] = jnp.where(diag, spread[16 * g : 16 * g + 16], 0.0).astype(BF16)
    wacc[...] = jnp.zeros_like(wacc)
    dwacc[...] = jnp.zeros_like(dwacc)
    points[...] = jnp.zeros_like(points)

    @pl.loop(0, S)
    def _(s):
        @pl.when(s < S - 2)
        def _():
            prepare(s + 2)
            pl.when(mine == s + 2)(send_cot)
            send_rims(fg, s + 2, f_send, f_recv)

        await_rims(fg, s, f_send, f_recv)

        @pl.when(s != mine)
        def _():
            cot_arrival(s).wait_recv()

        @pl.when(s == mine)
        def _():
            own_cot().wait()

        @pl.loop(0, 2, unroll=2)
        def _(pair_of):
            downs = []
            for jj in range(2):
                down = gdn[s, 2 * pair_of + jj]
                none = jnp.zeros_like(down)
                downs += [jnp.concatenate([down, none], axis=1), jnp.concatenate([none, down], axis=1)]
            downs = jnp.concatenate(downs, axis=0)
            gm_all = dot(w2t[...], downs, NT).astype(BF16)
            pools = ([], [], [], [])
            stacks = []
            lefts = [[], [], [], [], [], []]
            for jj in range(2):
                j = 2 * pair_of + jj
                gm_j = gm_all[:, 128 * jj : 128 * jj + 128]
                depth = conv(fg, mats, s, j)
                stacked = []
                for x in range(2):
                    dep = depth[x].astype(BF16)
                    gm_x = jnp.concatenate(
                        [gm_j[128 * x : 128 * x + 64], gm_j[128 * x + 64 : 128 * x + 128]], axis=1
                    )
                    pre_x, grad_x = dot(pin[...], dep), dot(pout_t[...], gm_x)
                    acts, gpres = [], []
                    for h in range(0, HID, 64):
                        pre, grad = pre_x[h : h + 64], grad_x[h : h + 64]
                        sq = pre * pre
                        t = jnp.tanh(pre * (G0 + G1 * sq))
                        up = 0.5 + 0.5 * t
                        acts.append((pre * up).astype(BF16))
                        slope = up + 0.5 * pre * (1.0 - t * t) * (G0 + 3 * G1 * sq)
                        gpres.append((grad * slope).astype(BF16))
                    act, gpre = jnp.concatenate(acts, axis=0), jnp.concatenate(gpres, axis=0)
                    own = jnp.concatenate(
                        [fg[s, 1 + x, 1 + 2 * j + yy].astype(F32) for yy in range(2)], axis=1
                    )
                    merged = (own + dot(pout[...], act)).astype(BF16)
                    stacked += [merged[:, :128], merged[:, 128:]]
                    for pool, part in zip(pools, (act, gm_x, gpre, dep)):
                        pool.append(part)
                    gdep = dot(pin_t[...], gpre).astype(BF16)
                    for yy in range(2):
                        part = gdep[:, 128 * yy : 128 * yy + 128]
                        dg[s, 1 + x, 1 + 2 * j + yy] = part
                        gm[s, x, 2 * j + yy] = gm_x[:, 128 * yy : 128 * yy + 128]
                        here = part.astype(F32)
                        none = jnp.zeros_like(here)
                        lefts[3 * x].append(shifted_sum(none, none, here).astype(BF16))
                        lefts[3 * x + 1].append(part)
                        lefts[3 * x + 2].append(shifted_sum(here, none, none).astype(BF16))
                stacked = jnp.concatenate(stacked, axis=0)
                mg[s, j] = stacked
                stacks.append(stacked)
            act, gm_x, gpre, dep = (jnp.concatenate(pool, axis=1) for pool in pools)
            points[0] += dot(act, gm_x, NT)
            points[1] += dot(gpre, dep, NT)
            term = dot(jnp.concatenate(stacks, axis=1), downs)
            wacc[256:512] += term[:, :128]
            wacc[512:768] += term[:, 128:]
            lines = [jnp.concatenate(line, axis=1) for line in lefts]
            for g in range(4):
                left = jnp.concatenate([m[16 * g : 16 * g + 16] for m in lines], axis=0)
                right = [taps(fg, s, 2 * pair_of + jj, g) for jj in range(2)]
                dwacc[g] += dot(left, jnp.concatenate(right, axis=1), NT)

        send_rims(dg, s, d_send, d_recv)

    spot = lax.broadcasted_iota(jnp.int32, (192, 128), 0)
    tap = lax.broadcasted_iota(jnp.int32, (192, 128), 1)
    picks, blocks = [], []
    for q in range(6):
        a = spot // 48 - q // 3
        picks.append(((tap == 9 * a + 3 * (spot // 16 % 3) + q % 3) & (a >= 0) & (a <= 2)).astype(BF16))
        blocks.append(
            jnp.concatenate([jnp.where(diag, dwacc[g, 16 * q : 16 * q + 16, :], 0.0) for g in range(4)], axis=0)
        )
    found = jnp.zeros((C, 128), F32)
    for q in range(6):
        high = blocks[q].astype(BF16)
        rest = blocks[q] - high.astype(F32)
        middle = rest.astype(BF16)
        low = (rest - middle.astype(F32)).astype(BF16)
        terms = dot(jnp.concatenate([high, middle, low], axis=0), picks[q])
        found += terms[:64] + terms[64:128] + terms[128:]
    wacc[768:832] = found
    wacc[0:256] = jnp.concatenate([points[0], points[1]], axis=1)

    def block(start, rows):
        return pl.ds(pl.multiple_of(start, 8), rows)

    def other(k):
        return (chip + k) % 8

    def pair_copy():
        give = block((1 - core) * HALF, HALF)
        return remote(wacc.at[give], pair, pair_send.at[0], pair_recv.at[0], (ix + 1 - 2 * core, iy))

    def rs_copy(k):
        give = block(core * HALF + other(k) * PART, PART)
        return remote(wacc.at[give], rs.at[chip], rs_send.at[k], rs_recv.at[8 - k], (2 * other(k) + core, iy))

    def rs_arrival(k):
        give = block(core * HALF, PART)
        return remote(wacc.at[give], rs.at[other(k)], rs_send.at[k], rs_recv.at[k], (ix, iy))

    def gy_copy(k):
        return remote(gyb.at[iy], gyb.at[iy], gy_send.at[k], gy_recv.at[NGY - k], (ix, (iy + k) % NGY))

    def gy_arrival(k):
        slot = (iy + k) % NGY
        return remote(gyb.at[slot], gyb.at[slot], gy_send.at[k], gy_recv.at[k], (ix, iy))

    def ag_copy(k):
        slot = core * 8 + chip
        return remote(tot.at[slot], tot.at[slot], ag_send.at[k], ag_recv.at[8 - k], (2 * other(k) + core, iy))

    def ag_arrival(k):
        slot = core * 8 + other(k)
        return remote(tot.at[slot], tot.at[slot], ag_send.at[k], ag_recv.at[k], (ix, iy))

    def last_copy():
        rows = pl.ds(core * 8, 8)
        return remote(tot.at[rows], tot.at[rows], pair_send.at[1], pair_recv.at[1], (ix + 1 - 2 * core, iy))

    def last_arrival():
        rows = pl.ds(8 - core * 8, 8)
        return remote(tot.at[rows], tot.at[rows], pair_send.at[1], pair_recv.at[1], (ix, iy))

    def total(buffer):
        result = buffer[0]
        for q in range(1, 8):
            result = result + buffer[q]
        return result

    pair_copy().start()

    def reduce(s):
        rows = jnp.concatenate([mg[s, j] for j in range(4)], axis=1)
        both = dot(rows, w2t[...], TN)
        for j in range(4):
            at = 128 * j
            red[s, j] = (both[at : at + 64, :128] + both[at + 64 : at + 128, 128:]).astype(BF16)

    def send_coarse(s):
        @pl.when(s != mine)
        def _():
            coarse_copy(s).start()

        @pl.when(s == mine)
        def _():
            own_coarse().start()

    for s in range(2):
        reduce(s)
    pair_copy().wait_recv()
    wacc[block(core * HALF, HALF)] += pair[...]
    for k in range(1, 8):
        rs_copy(k).start()
    for s in range(2):
        send_coarse(s)

    @pl.loop(0, S)
    def _(s):
        await_rims(dg, s, d_send, d_recv)

        @pl.loop(0, 4, unroll=2)
        def _(j):
            adjoint = conv(dg, mats_t, s, j)
            sides = []
            for x in range(2):
                for yy in range(2):
                    summed = gm[s, x, 2 * j + yy].astype(F32) + adjoint[x][:, 128 * yy : 128 * yy + 128]
                    sides.append(summed.astype(BF16))
            back = dot(jnp.concatenate(sides, axis=0), unperm)
            for x in range(2):
                for yy in range(2):
                    at = 128 * x + 64 * yy
                    swap[8 * x + 2 * j + yy] = back[at : at + 64]

        for h in range(4):
            turned = jnp.swapaxes(swap[:, 16 * h : 16 * h + 16, :], 0, 1)
            grad_out[s, 16 * h : 16 * h + 16] = turned.astype(BF16)
        store(s).start()

        @pl.when(s < 3)
        def _():
            for k in range(2):
                reduce(2 + 2 * s + k)
                send_coarse(2 + 2 * s + k)

        @pl.when(s == 2)
        def _():
            rs[chip] = wacc[block(core * HALF + chip * PART, PART)]
            for k in range(1, 8):
                rs_arrival(k).wait_recv()
            gyb[iy] = total(rs)
            for k in range(1, NGY):
                gy_copy(k).start()

        @pl.when(s == 4)
        def _():
            for k in range(1, NGY):
                gy_arrival(k).wait_recv()
            tot[core * 8 + chip] = (total(gyb) * SCALE).astype(BF16)
            for k in range(1, 8):
                ag_copy(k).start()

        @pl.when(s == 6)
        def _():
            for k in range(1, 8):
                ag_arrival(k).wait_recv()
            last_copy().start()

    last_arrival().wait_recv()
    for slot in range(16):
        flat[PART * slot : PART * slot + PART] = tot[slot].astype(F32)
    both = flat[0:256].T
    grad_po[...] = both[:64]
    grad_in[...] = both[64:]
    for k in range(8):
        at = 256 + 256 * (k % 2) + 64 * (k // 2)
        grad_down[pl.ds(k, 64, stride=8), :] = flat[at : at + 64]
    lines = flat[768:832].T
    for k in range(9):
        dw_out[k // 3, k % 3] = lines[3 * k : 3 * k + 3]

    own_coarse().wait()

    @pl.loop(0, S)
    def _(s):
        @pl.when(s != mine)
        def _():
            coarse_arrival(s).wait_recv()
            coarse_copy(s).wait_send()

        store(s).wait()
        for grid, send, recv in ((fg, f_send, f_recv), (dg, d_send, d_recv)):
            for goes, _, copy in rims(grid, s, send, recv):
                pl.when(goes)(copy.wait_send)

    for k in range(1, 8):
        cot_copy(k).wait_send()
        rs_copy(k).wait_send()
        ag_copy(k).wait_send()
        gy_copy(k).wait_send()
    pair_copy().wait_send()
    last_copy().wait_send()


def hand_over(*refs):
    held, arrive, leave = refs[12:18], refs[18], refs[19]
    trips = [(refs[1].at[s], held[1].at[s], refs[7].at[s]) for s in range(S)]
    trips += [(refs[n], held[n], refs[6 + n]) for n in (0, 2, 3, 4, 5)]
    into = [pltpu.make_async_copy(a, b, arrive.at[n]) for n, (a, b, _) in enumerate(trips)]
    out = [pltpu.make_async_copy(b, c, leave.at[n]) for n, (_, b, c) in enumerate(trips)]
    for copy in into:
        copy.start()
    for first, then in zip(into, out):
        first.wait()
        then.start()
    for copy in out:
        copy.wait()


def per_device(fields, depth_kernel, point_in, point_out, down_kernel, cotangent):
    raw = fields.reshape(S, C, 16, 128)
    cot = cotangent[0, 0, 0].transpose(1, 2, 3, 0)
    taps_in = depth_kernel.transpose(1, 2, 3, 0)
    down_in = down_kernel.transpose(1, 2, 3, 4, 0).reshape(8 * C, C2)
    vmem = pl.BlockSpec(memory_space=pltpu.VMEM)
    dma = pltpu.SemaphoreType.DMA
    hbm = pl.BlockSpec(memory_space=pl.ANY)
    results = pl.pallas_call(
        kernel,
        out_shape=(
            jax.ShapeDtypeStruct((4, 8, 64, 128), BF16),
            jax.ShapeDtypeStruct((S, C, 16, 128), BF16),
            jax.ShapeDtypeStruct((C, HID), F32),
            jax.ShapeDtypeStruct((C, HID), F32),
            jax.ShapeDtypeStruct((8 * C, C2), F32),
            jax.ShapeDtypeStruct((3, 3, 3, C), F32),
        ),
        in_specs=[hbm] * 2 + [vmem] * 4,
        out_specs=[vmem, hbm] + [vmem] * 4,
        scratch_shapes=[
            pltpu.VMEM((S, C, 16, 128), BF16),
            pltpu.VMEM((S, C, 16, 128), BF16),
            pltpu.VMEM((HID, C), BF16),
            pltpu.VMEM((HID, C), BF16),
            pltpu.VMEM((256, 256), BF16),
            pltpu.VMEM((8 * C, C2), F32),
            pltpu.VMEM((S, 4, 10, C, 128), BF16),
            pltpu.VMEM((S, 4, 10, C, 128), BF16),
            pltpu.VMEM((S, 2, 8, C, 128), BF16),
            pltpu.VMEM((S, 4, 256, 128), BF16),
            pltpu.VMEM((S, 4, 64, 128), BF16),
            pltpu.VMEM((S, 4, 64, 128), BF16),
            pltpu.VMEM((4, 96, 192), BF16),
            pltpu.VMEM((4, 96, 192), BF16),
            pltpu.VMEM((2 * HALF, 128), F32),
            pltpu.VMEM((4, 96, 192), F32),
            pltpu.VMEM((2, 256, 64), F32),
            pltpu.VMEM((16, C, 128), F32),
            pltpu.VMEM((HALF, 128), F32),
            pltpu.VMEM((8, PART, 128), F32),
            pltpu.VMEM((NGY, PART, 128), F32),
            pltpu.VMEM((16, PART, 128), BF16),
            pltpu.VMEM((2 * HALF, 128), F32),
            dma((S, 8)), dma((S, 8)), dma((S, 8)), dma((S, 8)),
            dma((8,)), dma((8,)), dma((8,)), dma((8,)),
            dma((8,)), dma((8,)), dma((NGY,)), dma((NGY,)), dma((8,)), dma((8,)), dma((2,)), dma((2,)),
            dma((2,)), dma((S,)), dma((S,)),
        ],
        compiler_params=pltpu.CompilerParams(
            collective_id=0, has_side_effects=True, vmem_limit_bytes=56 * 2**20
        ),
    )(raw, cot, taps_in, point_in.T, point_out, down_in)
    coarse, grad, grad_in, grad_po, grad_down, dw = pl.pallas_call(
        hand_over,
        out_shape=[jax.ShapeDtypeStruct(r.shape, r.dtype) for r in results],
        in_specs=[hbm] * 6,
        out_specs=[hbm] * 6,
        scratch_shapes=[pltpu.VMEM(r.shape, r.dtype) for r in results] + [dma((S + 5,)), dma((S + 5,))],
        compiler_params=pltpu.CompilerParams(vmem_limit_bytes=56 * 2**20),
        cost_estimate=pl.CostEstimate(flops=0, bytes_accessed=2**23, transcendentals=0),
    )(*results)
    coarse = coarse.transpose(3, 0, 1, 2)[None, None, None]
    grad_down = grad_down.reshape(C, 2, 2, 2, C2).transpose(4, 0, 1, 2, 3)
    dw = dw.transpose(3, 0, 1, 2)
    return coarse, grad.reshape(fields.shape), dw, grad_in.T, grad_po, grad_down


def solution(mesh):
    split = P("gx", "gy", None, None, None, None, None)
    fine = P(None, None, "gx", "gy", None)
    return jax.shard_map(
        per_device,
        mesh=mesh,
        in_specs=(fine, P(), P(), P(), P(), split),
        out_specs=(split, fine, P(), P(), P(), P()),
        check_vma=False,
    )
```

```python
import math

import jax
import jax.numpy as jnp
from jax import lax
from jax.experimental import pallas as pl
from jax.experimental.pallas import tpu as pltpu
from jax.sharding import PartitionSpec as P

NGX, NGY = 16, 8
S, C, HID, C2 = 8, 64, 256, 128
F32, BF16 = jnp.float32, jnp.bfloat16
MESH = pl.DeviceIdType.MESH
NN = (((1,), (0,)), ((), ()))
NT = (((1,), (1,)), ((), ()))
TN = (((0,), (0,)), ((), ()))
G0 = math.sqrt(2.0 / math.pi)
G1 = G0 * 0.044715
HALF, PART = 448, 56
SCALE = 1.0 / math.sqrt(8 * 32 * 64 * 128)


def dot(a, b, dims=NN):
    return lax.dot_general(a, b, dims, preferred_element_type=F32)


def taps(grid, s, j, g):
    sides = []
    for yy in range(2):
        block = grid[s, :, pl.ds(2 * j + yy, 3), 16 * g : 16 * g + 16, :]
        sides.append(block.reshape(192, 128))
    return jnp.concatenate(sides, axis=1)


def shifted_sum(a0, a1, a2):
    lane = lax.broadcasted_iota(jnp.int32, a1.shape, 1)
    low = lane < 64
    near = pltpu.roll(jnp.where(low, a0, a2), 64, 1)
    far = jnp.where(low, pltpu.roll(a0, 65, 1), pltpu.roll(a2, 63, 1))
    return a1 + near + jnp.where((lane == 0) | (lane == 127), 0.0, far)


def conv(grid, mats, s, j):
    parts = [dot(mats[g], taps(grid, s, j, g)) for g in range(4)]
    result = []
    for x in range(2):
        sides = []
        for yy in range(2):
            a = [
                jnp.concatenate(
                    [p[48 * x + 16 * e : 48 * x + 16 * e + 16, 128 * yy : 128 * yy + 128] for p in parts],
                    axis=0,
                )
                for e in range(3)
            ]
            sides.append(shifted_sum(*a))
        result.append(jnp.concatenate(sides, axis=1))
    return result


def kernel(
    raw_hbm, cot, taps_in, pin_t, pout, down_in,
    coarse, grad_hbm, grad_in, grad_po, grad_down, dw_out,
    raw, grad_out, pin, pout_t, w2t, wide,
    fg, dg, gm, mg, gdn, red, mats, mats_t, wacc, dwacc, points, swap, pair, rs, gyb, tot, flat,
    f_send, f_recv, d_send, d_recv, c_send, c_recv, r_send, r_recv,
    rs_send, rs_recv, gy_send, gy_recv, ag_send, ag_recv, pair_send, pair_recv, own_sem, in_sem, out_sem,
):
    ix, iy = lax.axis_index("gx"), lax.axis_index("gy")
    mx, my = ix % 4, iy % 2
    mine = mx * 2 + my
    bx, by = ix - mx, iy - my

    barrier = pltpu.get_barrier_semaphore()
    core, chip = ix % 2, ix // 2
    peers = [((ix + k) % NGX, iy) for k in range(2, NGX, 2)]
    peers += [(ix + 1 - 2 * core, iy), ((ix + NGX - 1 + 2 * core) % NGX, iy)]
    peers += [(ix, (iy + k) % NGY) for k in range(1, NGY)]
    peers += [((ix + p) % NGX, (iy + q) % NGY) for p in (1, NGX - 1) for q in (1, NGY - 1)]
    peers += [(bx + (mine + k) % 8 // 2, by + (mine + k) % 2) for k in range(1, 8)]
    for peer in peers:
        pl.semaphore_signal(barrier, inc=1, device_id=peer, device_id_type=MESH)

    def load(s):
        return pltpu.make_async_copy(raw_hbm.at[s], raw.at[s], in_sem.at[s])

    def store(s):
        return pltpu.make_async_copy(grad_out.at[s], grad_hbm.at[s], out_sem.at[s])

    for s in range(S):
        load(s).start()

    for grid in (fg, dg):
        for cond, at in ((ix == 0, 0), (ix == NGX - 1, 3)):

            @pl.when(cond)
            def _(grid=grid, at=at):
                @pl.loop(0, S)
                def _(s):
                    grid[s, at] = jnp.zeros((10, C, 128), BF16)

        for cond, at in ((iy == 0, 0), (iy == NGY - 1, 9)):

            @pl.when(cond)
            def _(grid=grid, at=at):
                @pl.loop(0, S)
                def _(s):
                    grid[s, :, at] = jnp.zeros((4, C, 128), BF16)

    def remote(src, dst, send, recv, to):
        return pltpu.make_async_remote_copy(
            src_ref=src, dst_ref=dst, send_sem=send, recv_sem=recv, device_id=to, device_id_type=MESH
        )

    def cot_copy(k):
        to = (mine + k) % 8
        tx, ty = to // 2, to % 2
        return remote(
            cot.at[tx, pl.ds(ty * 4, 4)], gdn.at[mine], c_send.at[to], c_recv.at[mine], (bx + tx, by + ty)
        )

    def cot_arrival(s):
        return remote(cot.at[0, pl.ds(0, 4)], gdn.at[s], c_send.at[s], c_recv.at[s], (ix, iy))

    def send_cot():
        for k in range(1, 8):
            cot_copy(k).start()

    def own_cot():
        return pltpu.make_async_copy(cot.at[mx, pl.ds(my * 4, 4)], gdn.at[mine], own_sem.at[1])

    own_cot().start()

    zi = lax.broadcasted_iota(jnp.int32, (128, 128), 0)
    li = lax.broadcasted_iota(jnp.int32, (128, 128), 1)
    perm = (zi == jnp.where(li < 64, 2 * li, 2 * li - 127)).astype(BF16)
    unperm = (li == jnp.where(zi < 64, 2 * zi, 2 * zi - 127)).astype(BF16)

    def rims(grid, s, send, recv):
        whole, inner = pl.ds(1, 8), pl.ds(1, 2)
        west, east, south, north = ix > 0, ix < NGX - 1, iy > 0, iy < NGY - 1
        listed = [
            (west, east, (ix - 1, iy), (1, whole), (3, whole)),
            (east, west, (ix + 1, iy), (2, whole), (0, whole)),
            (south, north, (ix, iy - 1), (inner, 1), (inner, 9)),
            (north, south, (ix, iy + 1), (inner, 8), (inner, 0)),
            (west & south, east & north, (ix - 1, iy - 1), (1, 1), (3, 9)),
            (west & north, east & south, (ix - 1, iy + 1), (1, 8), (3, 0)),
            (east & south, west & north, (ix + 1, iy - 1), (2, 1), (0, 9)),
            (east & north, west & south, (ix + 1, iy + 1), (2, 8), (0, 0)),
        ]
        return [
            (goes, comes, remote(grid.at[(s, *src)], grid.at[(s, *dst)], send.at[s, d], recv.at[s, d], to))
            for d, (goes, comes, to, src, dst) in enumerate(listed)
        ]

    def send_rims(grid, s, send, recv):
        for goes, _, copy in rims(grid, s, send, recv):
            pl.when(goes)(copy.start)

    def await_rims(grid, s, send, recv):
        for _, comes, copy in rims(grid, s, send, recv):
            pl.when(comes)(copy.wait_recv)

    def prepare(s):
        load(s).wait()
        for h in range(4):
            block = raw[s, 16 * h : 16 * h + 16].reshape(256, 128)
            turned = dot(block, perm).reshape(16, 16, 128)
            turned = jnp.swapaxes(turned, 0, 1).astype(BF16)
            for x in range(2):
                fg[s, 1 + x, 1:9, 16 * h : 16 * h + 16, :] = turned[8 * x : 8 * x + 8]

    def coarse_copy(s):
        return remote(
            red.at[s], coarse.at[mx, pl.ds(my * 4, 4)], r_send.at[s], r_recv.at[mine], (bx + s // 2, by + s % 2)
        )

    def coarse_arrival(s):
        return remote(
            red.at[s], coarse.at[s // 2, pl.ds(s % 2 * 4, 4)], r_send.at[s], r_recv.at[s], (ix, iy)
        )

    def own_coarse():
        return pltpu.make_async_copy(red.at[mine], coarse.at[mx, pl.ds(my * 4, 4)], own_sem.at[0])

    for s in range(2):
        prepare(s)
    pl.semaphore_wait(barrier, len(peers))
    pl.when(mine < 2)(send_cot)
    for s in range(2):
        send_rims(fg, s, f_send, f_recv)

    pin[...] = pin_t[...].astype(F32).T.astype(BF16)
    pout_t[...] = pout[...].astype(F32).T.astype(BF16)
    wide[...] = down_in[...].astype(F32)
    for k in range(8):
        at = 64 * (k // 2)
        w2t[at : at + 64, k % 2 * 128 : k % 2 * 128 + 128] = wide[pl.ds(k, 64, stride=8), :].astype(BF16)

    row = lax.broadcasted_iota(jnp.int32, (16, 192), 0)
    col = lax.broadcasted_iota(jnp.int32, (16, 192), 1)
    diag = row == col % 16
    tap = lax.broadcasted_iota(jnp.int32, (27, 192), 0)
    spot = lax.broadcasted_iota(jnp.int32, (27, 192), 1)
    given = taps_in[...].astype(F32)
    coefficients = jnp.concatenate([given[a, b] for a in range(3) for b in range(3)], axis=0).astype(BF16)
    for q in range(6):
        x, e = q // 3, q % 3
        a = spot // 48 - x
        at = 9 * a + 3 * (spot // 16 % 3) + e
        inside = (a >= 0) & (a <= 2)
        for to, place in ((mats, at), (mats_t, 26 - at)):
            spread = dot(coefficients, ((tap == place) & inside).astype(BF16), TN)
            for g in range(4):
                to[g, 16 * q : 16 * q + 16] = jnp.where(diag, spread[16 * g : 16 * g + 16], 0.0).astype(BF16)
    wacc[...] = jnp.zeros_like(wacc)
    dwacc[...] = jnp.zeros_like(dwacc)
    points[...] = jnp.zeros_like(points)

    @pl.loop(0, S)
    def _(s):
        @pl.when(s < S - 2)
        def _():
            prepare(s + 2)
            pl.when(mine == s + 2)(send_cot)
            send_rims(fg, s + 2, f_send, f_recv)

        await_rims(fg, s, f_send, f_recv)

        @pl.when(s != mine)
        def _():
            cot_arrival(s).wait_recv()

        @pl.when(s == mine)
        def _():
            own_cot().wait()

        @pl.loop(0, 2, unroll=2)
        def _(pair_of):
            downs = []
            for jj in range(2):
                down = gdn[s, 2 * pair_of + jj]
                none = jnp.zeros_like(down)
                downs += [jnp.concatenate([down, none], axis=1), jnp.concatenate([none, down], axis=1)]
            downs = jnp.concatenate(downs, axis=0)
            gm_all = dot(w2t[...], downs, NT).astype(BF16)
            pools = ([], [], [], [])
            stacks = []
            lefts = [[], [], [], [], [], []]
            for jj in range(2):
                j = 2 * pair_of + jj
                gm_j = gm_all[:, 128 * jj : 128 * jj + 128]
                depth = conv(fg, mats, s, j)
                stacked = []
                for x in range(2):
                    dep = depth[x].astype(BF16)
                    gm_x = jnp.concatenate(
                        [gm_j[128 * x : 128 * x + 64], gm_j[128 * x + 64 : 128 * x + 128]], axis=1
                    )
                    pre_x, grad_x = dot(pin[...], dep), dot(pout_t[...], gm_x)
                    acts, gpres = [], []
                    for h in range(0, HID, 64):
                        pre, grad = pre_x[h : h + 64], grad_x[h : h + 64]
                        sq = pre * pre
                        t = jnp.tanh(pre * (G0 + G1 * sq))
                        up = 0.5 + 0.5 * t
                        acts.append((pre * up).astype(BF16))
                        slope = up + 0.5 * pre * (1.0 - t * t) * (G0 + 3 * G1 * sq)
                        gpres.append((grad * slope).astype(BF16))
                    act, gpre = jnp.concatenate(acts, axis=0), jnp.concatenate(gpres, axis=0)
                    own = jnp.concatenate(
                        [fg[s, 1 + x, 1 + 2 * j + yy].astype(F32) for yy in range(2)], axis=1
                    )
                    merged = (own + dot(pout[...], act)).astype(BF16)
                    stacked += [merged[:, :128], merged[:, 128:]]
                    for pool, part in zip(pools, (act, gm_x, gpre, dep)):
                        pool.append(part)
                    gdep = dot(pin_t[...], gpre).astype(BF16)
                    for yy in range(2):
                        part = gdep[:, 128 * yy : 128 * yy + 128]
                        dg[s, 1 + x, 1 + 2 * j + yy] = part
                        gm[s, x, 2 * j + yy] = gm_x[:, 128 * yy : 128 * yy + 128]
                        here = part.astype(F32)
                        none = jnp.zeros_like(here)
                        lefts[3 * x].append(shifted_sum(none, none, here).astype(BF16))
                        lefts[3 * x + 1].append(part)
                        lefts[3 * x + 2].append(shifted_sum(here, none, none).astype(BF16))
                stacked = jnp.concatenate(stacked, axis=0)
                mg[s, j] = stacked
                stacks.append(stacked)
            act, gm_x, gpre, dep = (jnp.concatenate(pool, axis=1) for pool in pools)
            points[0] += dot(act, gm_x, NT)
            points[1] += dot(gpre, dep, NT)
            term = dot(jnp.concatenate(stacks, axis=1), downs)
            wacc[256:512] += term[:, :128]
            wacc[512:768] += term[:, 128:]
            lines = [jnp.concatenate(line, axis=1) for line in lefts]
            for g in range(4):
                left = jnp.concatenate([m[16 * g : 16 * g + 16] for m in lines], axis=0)
                right = [taps(fg, s, 2 * pair_of + jj, g) for jj in range(2)]
                dwacc[g] += dot(left, jnp.concatenate(right, axis=1), NT)

        send_rims(dg, s, d_send, d_recv)

    spot = lax.broadcasted_iota(jnp.int32, (192, 128), 0)
    tap = lax.broadcasted_iota(jnp.int32, (192, 128), 1)
    picks, blocks = [], []
    for q in range(6):
        a = spot // 48 - q // 3
        picks.append(((tap == 9 * a + 3 * (spot // 16 % 3) + q % 3) & (a >= 0) & (a <= 2)).astype(BF16))
        blocks.append(
            jnp.concatenate([jnp.where(diag, dwacc[g, 16 * q : 16 * q + 16, :], 0.0) for g in range(4)], axis=0)
        )
    found = jnp.zeros((C, 128), F32)
    for q in range(6):
        high = blocks[q].astype(BF16)
        rest = blocks[q] - high.astype(F32)
        middle = rest.astype(BF16)
        low = (rest - middle.astype(F32)).astype(BF16)
        terms = dot(jnp.concatenate([high, middle, low], axis=0), picks[q])
        found += terms[:64] + terms[64:128] + terms[128:]
    wacc[768:832] = found
    wacc[0:256] = jnp.concatenate([points[0], points[1]], axis=1)

    def block(start, rows):
        return pl.ds(pl.multiple_of(start, 8), rows)

    def other(k):
        return (chip + k) % 8

    def pair_copy():
        give = block((1 - core) * HALF, HALF)
        return remote(wacc.at[give], pair, pair_send.at[0], pair_recv.at[0], (ix + 1 - 2 * core, iy))

    def rs_copy(k):
        give = block(core * HALF + other(k) * PART, PART)
        return remote(wacc.at[give], rs.at[chip], rs_send.at[k], rs_recv.at[8 - k], (2 * other(k) + core, iy))

    def rs_arrival(k):
        give = block(core * HALF, PART)
        return remote(wacc.at[give], rs.at[other(k)], rs_send.at[k], rs_recv.at[k], (ix, iy))

    def gy_copy(k):
        return remote(gyb.at[iy], gyb.at[iy], gy_send.at[k], gy_recv.at[NGY - k], (ix, (iy + k) % NGY))

    def gy_arrival(k):
        slot = (iy + k) % NGY
        return remote(gyb.at[slot], gyb.at[slot], gy_send.at[k], gy_recv.at[k], (ix, iy))

    def ag_copy(k):
        slot = core * 8 + chip
        return remote(tot.at[slot], tot.at[slot], ag_send.at[k], ag_recv.at[8 - k], (2 * other(k) + core, iy))

    def ag_arrival(k):
        slot = core * 8 + other(k)
        return remote(tot.at[slot], tot.at[slot], ag_send.at[k], ag_recv.at[k], (ix, iy))

    def last_copy():
        rows = pl.ds(core * 8, 8)
        return remote(tot.at[rows], tot.at[rows], pair_send.at[1], pair_recv.at[1], (ix + 1 - 2 * core, iy))

    def last_arrival():
        rows = pl.ds(8 - core * 8, 8)
        return remote(tot.at[rows], tot.at[rows], pair_send.at[1], pair_recv.at[1], (ix, iy))

    def total(buffer):
        result = buffer[0]
        for q in range(1, 8):
            result = result + buffer[q]
        return result

    pair_copy().start()

    def reduce(s):
        rows = jnp.concatenate([mg[s, j] for j in range(4)], axis=1)
        both = dot(rows, w2t[...], TN)
        for j in range(4):
            at = 128 * j
            red[s, j] = (both[at : at + 64, :128] + both[at + 64 : at + 128, 128:]).astype(BF16)

    def send_coarse(s):
        @pl.when(s != mine)
        def _():
            coarse_copy(s).start()

        @pl.when(s == mine)
        def _():
            own_coarse().start()

    for s in range(2):
        reduce(s)
    pair_copy().wait_recv()
    wacc[block(core * HALF, HALF)] += pair[...]
    for k in range(1, 8):
        rs_copy(k).start()
    for s in range(2):
        send_coarse(s)

    @pl.loop(0, S)
    def _(s):
        await_rims(dg, s, d_send, d_recv)

        @pl.loop(0, 4, unroll=2)
        def _(j):
            adjoint = conv(dg, mats_t, s, j)
            sides = []
            for x in range(2):
                for yy in range(2):
                    summed = gm[s, x, 2 * j + yy].astype(F32) + adjoint[x][:, 128 * yy : 128 * yy + 128]
                    sides.append(summed.astype(BF16))
            back = dot(jnp.concatenate(sides, axis=0), unperm)
            for x in range(2):
                for yy in range(2):
                    at = 128 * x + 64 * yy
                    swap[8 * x + 2 * j + yy] = back[at : at + 64]

        for h in range(4):
            turned = jnp.swapaxes(swap[:, 16 * h : 16 * h + 16, :], 0, 1)
            grad_out[s, 16 * h : 16 * h + 16] = turned.astype(BF16)
        store(s).start()

        @pl.when(s < 3)
        def _():
            for k in range(2):
                reduce(2 + 2 * s + k)
                send_coarse(2 + 2 * s + k)

        @pl.when(s == 2)
        def _():
            rs[chip] = wacc[block(core * HALF + chip * PART, PART)]
            for k in range(1, 8):
                rs_arrival(k).wait_recv()
            gyb[iy] = total(rs)
            for k in range(1, NGY):
                gy_copy(k).start()

        @pl.when(s == 4)
        def _():
            for k in range(1, NGY):
                gy_arrival(k).wait_recv()
            tot[core * 8 + chip] = (total(gyb) * SCALE).astype(BF16)
            for k in range(1, 8):
                ag_copy(k).start()

        @pl.when(s == 7)
        def _():
            for k in range(1, 8):
                ag_arrival(k).wait_recv()
            last_copy().start()

    last_arrival().wait_recv()
    for slot in range(16):
        flat[PART * slot : PART * slot + PART] = tot[slot].astype(F32)
    both = flat[0:256].T
    grad_po[...] = both[:64]
    grad_in[...] = both[64:]
    for k in range(8):
        at = 256 + 256 * (k % 2) + 64 * (k // 2)
        grad_down[pl.ds(k, 64, stride=8), :] = flat[at : at + 64]
    lines = flat[768:832].T
    for k in range(9):
        dw_out[k // 3, k % 3] = lines[3 * k : 3 * k + 3]

    own_coarse().wait()

    @pl.loop(0, S)
    def _(s):
        @pl.when(s != mine)
        def _():
            coarse_arrival(s).wait_recv()
            coarse_copy(s).wait_send()

        store(s).wait()
        for grid, send, recv in ((fg, f_send, f_recv), (dg, d_send, d_recv)):
            for goes, _, copy in rims(grid, s, send, recv):
                pl.when(goes)(copy.wait_send)

    for k in range(1, 8):
        cot_copy(k).wait_send()
        rs_copy(k).wait_send()
        ag_copy(k).wait_send()
        gy_copy(k).wait_send()
    pair_copy().wait_send()
    last_copy().wait_send()


def hand_over(*refs):
    held, arrive, leave = refs[12:18], refs[18], refs[19]
    trips = [(refs[1].at[s], held[1].at[s], refs[7].at[s]) for s in range(S)]
    trips += [(refs[n], held[n], refs[6 + n]) for n in (0, 2, 3, 4, 5)]
    into = [pltpu.make_async_copy(a, b, arrive.at[n]) for n, (a, b, _) in enumerate(trips)]
    out = [pltpu.make_async_copy(b, c, leave.at[n]) for n, (_, b, c) in enumerate(trips)]
    for copy in into:
        copy.start()
    for first, then in zip(into, out):
        first.wait()
        then.start()
    for copy in out:
        copy.wait()


def per_device(fields, depth_kernel, point_in, point_out, down_kernel, cotangent):
    raw = fields.reshape(S, C, 16, 128)
    cot = cotangent[0, 0, 0].transpose(1, 2, 3, 0)
    taps_in = depth_kernel.transpose(1, 2, 3, 0)
    down_in = down_kernel.transpose(1, 2, 3, 4, 0).reshape(8 * C, C2)
    vmem = pl.BlockSpec(memory_space=pltpu.VMEM)
    dma = pltpu.SemaphoreType.DMA
    hbm = pl.BlockSpec(memory_space=pl.ANY)
    results = pl.pallas_call(
        kernel,
        out_shape=(
            jax.ShapeDtypeStruct((4, 8, 64, 128), BF16),
            jax.ShapeDtypeStruct((S, C, 16, 128), BF16),
            jax.ShapeDtypeStruct((C, HID), F32),
            jax.ShapeDtypeStruct((C, HID), F32),
            jax.ShapeDtypeStruct((8 * C, C2), F32),
            jax.ShapeDtypeStruct((3, 3, 3, C), F32),
        ),
        in_specs=[hbm] * 2 + [vmem] * 4,
        out_specs=[vmem, hbm] + [vmem] * 4,
        scratch_shapes=[
            pltpu.VMEM((S, C, 16, 128), BF16),
            pltpu.VMEM((S, C, 16, 128), BF16),
            pltpu.VMEM((HID, C), BF16),
            pltpu.VMEM((HID, C), BF16),
            pltpu.VMEM((256, 256), BF16),
            pltpu.VMEM((8 * C, C2), F32),
            pltpu.VMEM((S, 4, 10, C, 128), BF16),
            pltpu.VMEM((S, 4, 10, C, 128), BF16),
            pltpu.VMEM((S, 2, 8, C, 128), BF16),
            pltpu.VMEM((S, 4, 256, 128), BF16),
            pltpu.VMEM((S, 4, 64, 128), BF16),
            pltpu.VMEM((S, 4, 64, 128), BF16),
            pltpu.VMEM((4, 96, 192), BF16),
            pltpu.VMEM((4, 96, 192), BF16),
            pltpu.VMEM((2 * HALF, 128), F32),
            pltpu.VMEM((4, 96, 192), F32),
            pltpu.VMEM((2, 256, 64), F32),
            pltpu.VMEM((16, C, 128), F32),
            pltpu.VMEM((HALF, 128), F32),
            pltpu.VMEM((8, PART, 128), F32),
            pltpu.VMEM((NGY, PART, 128), F32),
            pltpu.VMEM((16, PART, 128), BF16),
            pltpu.VMEM((2 * HALF, 128), F32),
            dma((S, 8)), dma((S, 8)), dma((S, 8)), dma((S, 8)),
            dma((8,)), dma((8,)), dma((8,)), dma((8,)),
            dma((8,)), dma((8,)), dma((NGY,)), dma((NGY,)), dma((8,)), dma((8,)), dma((2,)), dma((2,)),
            dma((2,)), dma((S,)), dma((S,)),
        ],
        compiler_params=pltpu.CompilerParams(
            collective_id=0, has_side_effects=True, vmem_limit_bytes=56 * 2**20
        ),
    )(raw, cot, taps_in, point_in.T, point_out, down_in)
    coarse, grad, grad_in, grad_po, grad_down, dw = pl.pallas_call(
        hand_over,
        out_shape=[jax.ShapeDtypeStruct(r.shape, r.dtype) for r in results],
        in_specs=[hbm] * 6,
        out_specs=[hbm] * 6,
        scratch_shapes=[pltpu.VMEM(r.shape, r.dtype) for r in results] + [dma((S + 5,)), dma((S + 5,))],
        compiler_params=pltpu.CompilerParams(vmem_limit_bytes=56 * 2**20),
        cost_estimate=pl.CostEstimate(flops=0, bytes_accessed=2**23, transcendentals=0),
    )(*results)
    coarse = coarse.transpose(3, 0, 1, 2)[None, None, None]
    grad_down = grad_down.reshape(C, 2, 2, 2, C2).transpose(4, 0, 1, 2, 3)
    dw = dw.transpose(3, 0, 1, 2)
    return coarse, grad.reshape(fields.shape), dw, grad_in.T, grad_po, grad_down


def solution(mesh):
    split = P("gx", "gy", None, None, None, None, None)
    fine = P(None, None, "gx", "gy", None)
    return jax.shard_map(
        per_device,
        mesh=mesh,
        in_specs=(fine, P(), P(), P(), P(), split),
        out_specs=(split, fine, P(), P(), P(), P()),
        check_vma=False,
    )
```
